256 devices in a mesh: gx: 8 (over x, core), gy: 32 (over z, y).
Axes of the slice: x: 4, y: 4, z: 8, core: 2. Of those that a mesh axis runs over, the one named last changes fastest.
Arguments:
- charges: bfloat16 [524288, 32], P(('gx', 'gy')), may hold values from -6 to 6
- panel_counts: int32 [8192], P(('gx', 'gy')), may hold values from 1 to 64, as said below
- basis: bfloat16 [8192, 64, 64], P(('gx', 'gy')), may hold values from -0.75 to 0.75
- transfer: bfloat16 [8192, 64, 64], P(('gx', 'gy')), may hold values from -0.5 to 0.5
- leaf_coupling: bfloat16 [8192, 16, 64, 64], P(('gx', 'gy')), may hold values from -0.1875 to 0.1875
- leaf_partners: int32 [8192, 16], P(('gx', 'gy')), may hold values from 0 to 8191, as said below
- near_blocks: bfloat16 [8192, 3, 64, 64], P(('gx', 'gy')), may hold values from -0.4375 to 0.4375
- parent_coupling: bfloat16 [4096, 16, 64, 64], P(('gx', 'gy')), may hold values from -0.1875 to 0.1875
- parent_partners: int32 [4096, 16], P(('gx', 'gy')), may hold values from 0 to 4095, as said below
Outputs:
- potential: bfloat16 [524288, 32], P(('gx', 'gy'))
The draws below stay inside these ranges and needn't reach their ends.
Inputs may be any that keep to these rules, and one draw needn't show every extreme that they name: `panel_counts`: every value 1 to 64 occurs; every fifth leaf has all 64 panels live. `leaf_partners`: the partner of leaf g lies among the leaves of g's device, the device before or the device after in the order of the combined index gx * 32 + gy (leaf g is on device g // 32). `parent_partners`: the partner of parent q lies in the same block of 512 parents as q (one index of gx).
All inputs are finite; a program needn't handle non-finite values.
Results may differ from the reference program's by a relative error of at most 0.0054.
Values may be sent and summed in bfloat16 or wider, within the bound.
A program may use at most 128 MiB of HBM per device.

```python
import jax
import jax.numpy as jnp
from jax import lax

LEAF = 64
K = 64
R = 32
NC = 16
NC2 = 16
LD = 32
LEAVES = 8192
PARENTS = 4096
ROWP = 512
PANELS = 524288
DEVICES = 256


def draw_panel_counts(key, part):
    key = jax.random.fold_in(key, 1)
    counts = jax.random.randint(key, (LEAVES,), 1, LEAF + 1)
    counts = counts.at[::5].set(LEAF)
    return counts.astype(jnp.int32)


def draw_leaf_partners(key, part):
    key = jax.random.fold_in(key, 2)
    owner = jnp.arange(LEAVES, dtype=jnp.int32) // LD
    offset = jax.random.randint(key, (LEAVES, NC), -LD, 2 * LD)
    chosen = owner[:, None] * LD + offset
    return jnp.clip(chosen, 0, LEAVES - 1).astype(jnp.int32)


def draw_parent_partners(key, part):
    key = jax.random.fold_in(key, 3)
    block = jnp.arange(PARENTS, dtype=jnp.int32) // ROWP
    offset = jax.random.randint(key, (PARENTS, NC2), 0, ROWP)
    return (block[:, None] * ROWP + offset).astype(jnp.int32)


def shard_levels(key, dims, shards, smallest, top_value):
    level, own = 1.0, jax.random.fold_in(key, 6)
    for position, blocks in shards:
        draws = jnp.exp(jax.random.uniform(jax.random.fold_in(own, position), (blocks,), jnp.float32, smallest / len(shards), top_value / len(shards)))
        level = level * jnp.repeat(draws, dims[position] // blocks).reshape([-1 if axis == position else 1 for axis in range(len(dims))])
    return level


def gaussian(stream_key, shape, scale, bound, cuts=(), held_as=jnp.bfloat16):
    result = scale * jax.random.normal(stream_key, shape, jnp.float32)
    if cuts:
        result = result * shard_levels(stream_key, shape, cuts, -0.22, 0.18)
    return jnp.clip(result, -bound, bound).astype(held_as)


def setup_inputs(seed: int = 0) -> dict:
    key_list = jax.random.split(jax.random.key(seed), 10)
    charges = gaussian(key_list[0], (PANELS, R), 1.0, 6.0, ((0, 256),))
    panel_counts = draw_panel_counts(jax.random.fold_in(key_list[9], 71), 0)
    basis = gaussian(key_list[2], (LEAVES, LEAF, K), LEAF ** -0.5, 0.75, ((0, 256),))
    transfer = gaussian(key_list[3], (LEAVES, K, K), (2 * K) ** -0.5, 0.5, ((0, 256),))
    leaf_coupling = gaussian(key_list[4], (LEAVES, NC, K, K), (NC * K) ** -0.5, 0.1875, ((0, 256),))
    leaf_partners = draw_leaf_partners(jax.random.fold_in(key_list[9], 71), 0)
    near_blocks = gaussian(key_list[6], (LEAVES, 3, LEAF, LEAF), (3 * LEAF) ** -0.5, 0.4375, ((0, 256),))
    parent_coupling = gaussian(key_list[7], (PARENTS, NC2, K, K), (NC2 * K) ** -0.5, 0.1875, ((0, 256),))
    parent_partners = draw_parent_partners(jax.random.fold_in(key_list[9], 71), 0)
    return {"charges": charges, "panel_counts": panel_counts, "basis": basis, "transfer": transfer, "leaf_coupling": leaf_coupling, "leaf_partners": leaf_partners, "near_blocks": near_blocks, "parent_coupling": parent_coupling, "parent_partners": parent_partners}


def reference(charges, panel_counts, basis, transfer, leaf_coupling, leaf_partners, near_blocks, parent_coupling, parent_partners):
    slots = jnp.arange(LEAF, dtype=jnp.int32)
    mask = (slots[None, :] < panel_counts[:, None]).astype(jnp.bfloat16)[:, :, None]
    live = charges.reshape(LEAVES, LEAF, R) * mask
    leaf_coef = jnp.einsum('gpk,gpr->gkr', basis.astype(jnp.float32), live.astype(jnp.float32)).astype(jnp.bfloat16)
    pairs = transfer.reshape(PARENTS, 2, K, K).astype(jnp.float32)
    kids = leaf_coef.reshape(PARENTS, 2, K, R).astype(jnp.float32)
    parent_coef = jnp.einsum('qckl,qckr->qlr', pairs, kids).astype(jnp.bfloat16)

    def parent_block(args):
        blocks, partners = args
        picked = parent_coef[partners].astype(jnp.float32)
        return jnp.einsum('qjkl,qjlr->qkr', blocks.astype(jnp.float32), picked)

    half = LD // 2
    parent_far = lax.map(parent_block, (parent_coupling.reshape(DEVICES, half, NC2, K, K), parent_partners.reshape(DEVICES, half, NC2)))
    parent_far = parent_far.reshape(PARENTS, K, R).astype(jnp.bfloat16)
    spread = jnp.repeat(parent_far, 2, axis=0).astype(jnp.float32)
    zero_leaf = jnp.zeros((1, LEAF, R), jnp.bfloat16)
    padded = jnp.concatenate([zero_leaf, live, zero_leaf], axis=0)

    def leaf_block(args):
        blocks, partners, trans, near_b, bas, down, start = args
        picked = leaf_coef[partners].astype(jnp.float32)
        far = jnp.einsum('gjkl,gjlr->gkr', blocks.astype(jnp.float32), picked)
        local_coef = (far + jnp.einsum('gkl,glr->gkr', trans.astype(jnp.float32), down)).astype(jnp.bfloat16)
        window = lax.dynamic_slice_in_dim(padded, start, LD + 2, 0).astype(jnp.float32)
        near = jnp.zeros((LD, LEAF, R), jnp.float32)
        for n in range(3):
            near = near + jnp.einsum('gpq,gqr->gpr', near_b[:, n].astype(jnp.float32), window[n:n + LD])
        return jnp.einsum('gpk,gkr->gpr', bas.astype(jnp.float32), local_coef.astype(jnp.float32)) + near

    starts = jnp.arange(DEVICES, dtype=jnp.int32) * LD
    total = lax.map(leaf_block, (leaf_coupling.reshape(DEVICES, LD, NC, K, K), leaf_partners.reshape(DEVICES, LD, NC), transfer.reshape(DEVICES, LD, K, K), near_blocks.reshape(DEVICES, LD, 3, LEAF, LEAF), basis.reshape(DEVICES, LD, LEAF, K), spread.reshape(DEVICES, LD, K, R), starts))
    total = total.reshape(LEAVES, LEAF, R) * mask.astype(jnp.float32)
    return total.astype(jnp.bfloat16).reshape(PANELS, R)
```

```python
import jax
import jax.numpy as jnp
from jax import lax
from jax.experimental import pallas as pl
from jax.experimental.pallas import tpu as pltpu
from jax.sharding import PartitionSpec as P

BF = jnp.bfloat16
F32 = jnp.float32
MESH = pl.DeviceIdType.MESH

NY = 4
NZ = 8
NGX = 8
NGY = NY * NZ
LD = 32
QD = 16
TD = QD // 2
ROW_TILES = NGY * TD
R = 32
WIN = 4

SPAN = {"A": (0, 4), "A0": (0, 2), "A1": (2, 2), "B": (4, 4), "B0": (4, 2), "B1": (6, 2)}


def children(dy, dz, part):
    out = []
    if part == "A":
        if dz == 0:
            if dy == 0:
                out += [("y+", 1, 0, "A"), ("y-", -1, 0, "A")]
            if dy == 1:
                out += [("y+", 2, 0, "A0")]
            if dy == -1:
                out += [("y-", 2, 0, "A1")]
            out += [("z+", dy, 1, "A"), ("z-", dy, -1, "A")]
        elif dz in (1, 2):
            out += [("z+", dy, dz + 1, "A")]
        elif dz in (-1, -2):
            out += [("z-", dy, dz - 1, "A")]
        elif dz == 3:
            out += [("z+", dy, 4, "A0")]
        elif dz == -3:
            out += [("z-", dy, 4, "A1")]
    if part == "B":
        if dy == 0:
            if dz in (0, 1, 2):
                out += [("z+", 0, dz + 1, "B")]
            if dz in (0, -1, -2):
                out += [("z-", 0, dz - 1, "B")]
            if dz == 3:
                out += [("z+", 0, 4, "B0")]
            if dz == -3:
                out += [("z-", 0, 4, "B1")]
            out += [("y+", 1, dz, "B"), ("y-", -1, dz, "B")]
        elif dy == 1:
            out += [("y+", 2, dz, "B0")]
        elif dy == -1:
            out += [("y-", 2, dz, "B1")]
    return out


STEPS = (
    ((1, 0, "A"),), ((-1, 0, "A"),), ((0, 1, "B"),), ((0, -1, "B"),),
    ((1, 0, "B"),), ((-1, 0, "B"),), ((0, 1, "A"),), ((0, -1, "A"),),
    ((1, 1, "A"),), ((1, -1, "A"),), ((-1, 1, "A"),), ((-1, -1, "A"),),
    ((0, 2, "B"),), ((0, -2, "B"),), ((2, 0, "A0"), (2, 0, "A1")),
    ((0, 2, "A"),), ((0, -2, "A"),), ((1, 1, "B"),), ((-1, 1, "B"),),
    ((1, 2, "A"),), ((1, -2, "A"),), ((1, -1, "B"),), ((-1, -1, "B"),),
    ((-1, 2, "A"),), ((-1, -2, "A"),), ((2, 0, "B0"), (2, 0, "B1")),
    ((0, 3, "B"),), ((0, -3, "B"),), ((1, 2, "B"),), ((-1, 2, "B"),),
    ((2, 1, "A"),), ((2, -1, "A"),), ((1, -2, "B"),), ((-1, -2, "B"),),
    ((2, 1, "B0"), (2, 1, "B1")), ((0, 3, "A"),), ((0, -3, "A"),),
    ((2, -1, "B0"), (2, -1, "B1")), ((1, 3, "A"),), ((1, -3, "A"),),
    ((1, 3, "B"),), ((-1, 3, "B"),), ((-1, 3, "A"),), ((-1, -3, "A"),),
    ((1, -3, "B"),), ((-1, -3, "B"),), ((0, 4, "B0"), (0, 4, "B1")),
    ((2, 2, "B0"), (2, 2, "B1")), ((2, -2, "B0"), (2, -2, "B1")),
    ((2, 2, "A"),), ((2, -2, "A"),), ((2, 3, "B0"), (2, 3, "B1")),
    ((0, 4, "A0"), (0, 4, "A1")), ((1, 4, "A0"), (1, 4, "A1")),
    ((2, -3, "B0"), (2, -3, "B1")), ((-1, 4, "A0"), (-1, 4, "A1")),
    ((1, 4, "B"),), ((-1, 4, "B"),), ((2, 3, "A"),), ((2, -3, "A"),),
    ((2, 4, "B0"), (2, 4, "B1")), ((2, 4, "A0"), (2, 4, "A1")),
)
MESSAGES = tuple(m for step in STEPS for m in step)
NUMBER = {m: i for i, m in enumerate(MESSAGES)}


def dot_nn(a, b):
    return lax.dot_general(a, b, (((1,), (0,)), ((), ())), preferred_element_type=F32)


def dot_nt(a, b):
    return lax.dot_general(a, b, (((1,), (1,)), ((), ())), preferred_element_type=F32)


def kernel(
    ch_hbm, cnt_hbm, basis_hbm, transfer_hbm, lc_hbm, lp_hbm, nb_hbm, pc_hbm, pp_hbm,
    out_ref,
    ch, basis, transfer, lc, nb, pc, cnt, lp, pp,
    live, win, row, cpl, bdiag, near, far,
    in_sem, recv_sem, send_sem, rim_recv, rim_send,
):
    gx = lax.axis_index("gx")
    gy = lax.axis_index("gy")
    z = gy // NY
    y = gy % NY
    dev = gx * NGY + gy
    total = NGX * NGY
    prv = (dev + total - 1) % total
    nxt = (dev + 1) % total
    prv_id = (prv // NGY, prv % NGY)
    nxt_id = (nxt // NGY, nxt % NGY)
    ids = {
        "y+": (gx, z * NY + (y + 1) % NY),
        "y-": (gx, z * NY + (y + NY - 1) % NY),
        "z+": (gx, ((z + 1) % NZ) * NY + y),
        "z-": (gx, ((z + NZ - 1) % NZ) * NY + y),
    }

    loads = [
        pltpu.make_async_copy(s, d, in_sem.at[i])
        for i, (s, d) in enumerate(
            [
                (ch_hbm, ch), (cnt_hbm, cnt), (basis_hbm, basis), (transfer_hbm, transfer),
                (nb_hbm, nb), (lp_hbm, lp), (pp_hbm, pp), (lc_hbm, lc), (pc_hbm, pc),
            ]
        )
    ]
    for load in loads:
        load.start()

    barrier = pltpu.get_barrier_semaphore()
    for d in (ids["y+"], ids["y-"], ids["z+"], ids["z-"], prv_id, nxt_id):
        pl.semaphore_signal(barrier, inc=1, device_id=d, device_id_type=MESH)

    mine, before, after = ((d % WIN) * QD for d in (dev, prv, nxt))

    lane = lax.broadcasted_iota(jnp.int32, (R, 128), 1)
    low = lane < 64

    def masks(q):
        return lane < cnt[2 * q], (lane >= 64) & (lane < cnt[2 * q + 1] + 64)

    def swap(tile):
        return jnp.concatenate([tile[:, 64:], tile[:, :64]], axis=1)

    for load in loads[:4]:
        load.wait()

    zero = jnp.zeros((R, 128), BF)
    parents = []
    for q in range(QD):
        m0, m1 = masks(q)
        tile = ch[:, 128 * q : 128 * q + 128]
        l0 = jnp.where(m0, tile, zero)
        l1 = jnp.where(m1, tile, zero)
        live[q + 1] = l0 + l1
        coef = dot_nn(jnp.concatenate([l0, l1], axis=0), basis[2 * q : 2 * q + 2].reshape(128, 64))
        coef = coef.astype(BF)
        pair = jnp.concatenate([coef[:R], coef[R:]], axis=1)
        win[0, mine + q] = pair
        win[1, mine + q] = jnp.concatenate([coef[R:], coef[:R]], axis=1)
        parents.append(dot_nn(pair, transfer[2 * q : 2 * q + 2].reshape(128, 64)).astype(BF))
        if q % 2:
            a, b = parents[q - 1], parents[q]
            row[0, gy * TD + q // 2] = jnp.concatenate([a, b], axis=1)
            row[1, gy * TD + q // 2] = jnp.concatenate([b, a], axis=1)

    pl.semaphore_wait(barrier, 6)

    def slot(dy, dz, part):
        start, size = SPAN[part]
        origin = ((z + (NZ - dz)) % NZ) * NY + (y + (NY - dy)) % NY
        return row.at[0, pl.ds(origin * TD + start, size)]

    def send(src, m, direction):
        part = m[2]
        ref = slot(src[0], src[1], part)
        pltpu.make_async_remote_copy(
            src_ref=ref, dst_ref=ref, send_sem=send_sem, recv_sem=recv_sem.at[NUMBER[m]],
            device_id=ids[direction], device_id_type=MESH,
        ).start()

    def receive(m):
        ref = slot(*m)
        pltpu.make_async_remote_copy(
            src_ref=ref, dst_ref=ref, send_sem=send_sem, recv_sem=recv_sem.at[NUMBER[m]],
            device_id=ids["y+"], device_id_type=MESH,
        ).wait_recv()

    for d, dy, dz, part in (
        ("y+", 1, 0, "A"), ("y-", -1, 0, "A"), ("z+", 0, 1, "B"), ("z-", 0, -1, "B"),
        ("y+", 1, 0, "B"), ("y-", -1, 0, "B"), ("z+", 0, 1, "A"), ("z-", 0, -1, "A"),
    ):
        send((0, 0), (dy, dz, part), d)

    own = win.at[0, pl.ds(mine, QD)]
    rims = [
        pltpu.make_async_remote_copy(
            src_ref=s, dst_ref=d, send_sem=rim_send.at[i], recv_sem=rim_recv.at[i],
            device_id=to, device_id_type=MESH,
        )
        for i, (s, d, to) in enumerate(
            [
                (own, own, nxt_id),
                (own, own, prv_id),
                (live.at[pl.ds(QD, 1)], live.at[pl.ds(0, 1)], nxt_id),
                (live.at[pl.ds(1, 1)], live.at[pl.ds(QD + 1, 1)], prv_id),
            ]
        )
    ]
    for rim in rims:
        rim.start()

    def do_diag(q):
        b0, b1 = basis[2 * q], basis[2 * q + 1]
        o = jnp.zeros((64, 64), BF)
        bdiag[q, :64] = jnp.concatenate([b0, o], axis=1)
        bdiag[q, 64:] = jnp.concatenate([o, b1], axis=1)

    def do_near(q):
        o = jnp.zeros((64, 64), BF)
        o2 = jnp.zeros((64, 128), BF)
        top = jnp.concatenate([o, nb[2 * q, 0], nb[2 * q, 1], nb[2 * q, 2], o2], axis=1)
        low_rows = jnp.concatenate(
            [o2, nb[2 * q + 1, 0], nb[2 * q + 1, 1], nb[2 * q + 1, 2], o], axis=1
        )
        lhs = jnp.concatenate([live[q], live[q + 1], live[q + 2]], axis=1)
        near[q] = dot_nt(lhs, jnp.concatenate([top, low_rows], axis=0))

    def do_couple(q):
        for i in range(8):
            cpl[q, :, 128 * i : 128 * i + 128] = jnp.concatenate(
                [pc[q, 2 * i], pc[q, 2 * i + 1]], axis=1
            )

    def pick(ref, p, q):
        tiles = ref.shape[1]
        a = ref[p & 1, (p >> 1) & (tiles - 1)]
        b = ref[1 - (q & 1), (q >> 1) & (tiles - 1)]
        return jnp.where(low, a, b)

    def leaf_sum(g):
        lhs = jnp.concatenate(
            [pick(win, lp[2 * i, g], lp[2 * i + 1, g]) for i in range(8)], axis=1
        )
        rhs = jnp.concatenate([lc[g, j] for j in range(16)], axis=1)
        return dot_nt(lhs, rhs)

    def do_far(q):
        far[q] = jnp.concatenate([leaf_sum(2 * q), leaf_sum(2 * q + 1)], axis=1)

    def take_rims():
        for rim in rims:
            rim.wait_recv()
        live[0] = jnp.where(dev > 0, live[0], zero)
        live[QD + 1] = jnp.where(dev < total - 1, live[QD + 1], zero)

        @pl.loop(0, QD)
        def _(t):
            win[1, before + t] = swap(win[0, before + t])
            win[1, after + t] = swap(win[0, after + t])

    def wait_load(i):
        return loads[i].wait

    work = [lambda q=q: do_diag(q) for q in range(QD)]
    work += [wait_load(4)] + [lambda q=q: do_near(q) for q in range(1, QD - 1)]
    work += [wait_load(8)] + [lambda q=q: do_couple(q) for q in range(QD)]
    work += [wait_load(5), wait_load(7), take_rims]
    work += [lambda: do_near(0), lambda: do_near(QD - 1)]
    work += [lambda q=q: do_far(q) for q in range(QD)]
    done = 0
    for s, step in enumerate(STEPS):
        for m in step:
            receive(m)
        dy, dz, part = step[0]
        for d, ny, nz, np_ in children(dy, dz, part[0] if len(step) == 2 else part):
            send((dy, dz), (ny, nz, np_), d)
        upto = min(len(work), (s + 1) * len(work) // (len(STEPS) - 6))
        for unit in work[done:upto]:
            unit()
        done = upto
        for m in step:
            start, size = SPAN[m[2]]
            origin = ((z + (NZ - dz)) % NZ) * NY + (y + (NY - dy)) % NY
            for t in range(size):
                at = origin * TD + start + t
                row[1, at] = swap(row[0, at])

    loads[6].wait()
    for q in range(QD):
        lhs = jnp.concatenate(
            [pick(row, pp[q, 2 * i], pp[q, 2 * i + 1]) for i in range(8)], axis=1
        )
        parent_far = dot_nt(lhs, cpl[q]).astype(BF)
        local = dot_nt(parent_far, transfer[2 * q : 2 * q + 2].reshape(128, 64)) + far[q]
        total_q = dot_nt(local.astype(BF), bdiag[q]) + near[q]
        m0, m1 = masks(q)
        out_ref[:, 128 * q : 128 * q + 128] = jnp.where(m0 | m1, total_q, 0.0).astype(BF)

    for rim in rims:
        rim.wait_send()
    sent = row.at[0, pl.ds(0, ROW_TILES - TD)]
    pltpu.make_async_remote_copy(
        src_ref=sent, dst_ref=sent, send_sem=send_sem, recv_sem=recv_sem.at[0],
        device_id=ids["y+"], device_id_type=MESH,
    ).wait_send()


def per_device(
    charges, panel_counts, basis, transfer, leaf_coupling, leaf_partners, near_blocks,
    parent_coupling, parent_partners,
):
    n = charges.shape[0]
    result = pl.pallas_call(
        kernel,
        out_shape=jax.ShapeDtypeStruct((R, n), BF),
        in_specs=[pl.BlockSpec(memory_space=pltpu.HBM)] * 9,
        out_specs=pl.BlockSpec(memory_space=pltpu.VMEM),
        scratch_shapes=[
            pltpu.VMEM((R, n), BF),
            pltpu.VMEM(basis.shape, BF),
            pltpu.VMEM(transfer.shape, BF),
            pltpu.VMEM(leaf_coupling.shape, BF),
            pltpu.VMEM(near_blocks.shape, BF),
            pltpu.VMEM(parent_coupling.shape, BF),
            pltpu.SMEM((LD,), jnp.int32),
            pltpu.SMEM((16, LD), jnp.int32),
            pltpu.SMEM((QD, 16), jnp.int32),
            pltpu.VMEM((QD + 2, R, 128), BF),
            pltpu.VMEM((2, WIN * QD, R, 128), BF),
            pltpu.VMEM((2, ROW_TILES, R, 128), BF),
            pltpu.VMEM((QD, 64, 1024), BF),
            pltpu.VMEM((QD, 128, 128), BF),
            pltpu.VMEM((QD, R, 128), F32),
            pltpu.VMEM((QD, R, 128), F32),
            pltpu.SemaphoreType.DMA((9,)),
            pltpu.SemaphoreType.DMA((len(MESSAGES),)),
            pltpu.SemaphoreType.DMA,
            pltpu.SemaphoreType.DMA((4,)),
            pltpu.SemaphoreType.DMA((4,)),
        ],
        compiler_params=pltpu.CompilerParams(
            collective_id=0, has_side_effects=True, vmem_limit_bytes=56 * 1024 * 1024
        ),
    )(
        charges.T, panel_counts, basis, transfer, leaf_coupling, leaf_partners.T, near_blocks,
        parent_coupling, parent_partners,
    )
    return result.T


def solution(mesh):
    in_specs = (
        P(("gx", "gy"), None),
        P(("gx", "gy")),
        P(("gx", "gy"), None, None),
        P(("gx", "gy"), None, None),
        P(("gx", "gy"), None, None, None),
        P(("gx", "gy"), None),
        P(("gx", "gy"), None, None, None),
        P(("gx", "gy"), None, None, None),
        P(("gx", "gy"), None),
    )
    out_specs = P(("gx", "gy"), None)
    return jax.shard_map(
        per_device, mesh=mesh, in_specs=in_specs, out_specs=out_specs, check_vma=False
    )
```

```python
import jax
import jax.numpy as jnp
from jax import lax
from jax.experimental import pallas as pl
from jax.experimental.pallas import tpu as pltpu
from jax.sharding import PartitionSpec as P

BF = jnp.bfloat16
F32 = jnp.float32
MESH = pl.DeviceIdType.MESH

NY = 4
NZ = 8
NGX = 8
NGY = NY * NZ
LD = 32
QD = 16
UD = QD
ROW_UNITS = NGY * UD
R = 32
WIN = 4

SPAN = {"A": (0, 6), "A0": (0, 3), "A1": (3, 3), "B": (6, 10), "B0": (6, 5), "B1": (11, 5)}

ROUTES = {
    (0, 0, "A"): (
        ("y+", 2, (2, 0, "A0")),
        ("y-", 2, (2, 0, "A1")),
        ("y+", 1, (1, 0, "A")),
        ("y-", 1, (-1, 0, "A")),
        ("z+", 1, (0, 1, "A")),
        ("z-", 1, (0, -1, "A")),
    ),
    (0, 0, "B"): (
        ("z+", 2, (0, 2, "B")),
        ("z+", 1, (0, 1, "B")),
        ("z-", 2, (0, -2, "B")),
        ("z-", 1, (0, -1, "B")),
        ("y+", 1, (1, 0, "B")),
        ("y-", 1, (-1, 0, "B")),
    ),
    (0, 1, "A"): (
        ("z+", 1, (0, 2, "A")),
    ),
    (0, -1, "A"): (
        ("z-", 1, (0, -2, "A")),
    ),
    (1, 0, "A"): (
        ("z+", 1, (1, 1, "A")),
        ("z-", 1, (1, -1, "A")),
    ),
    (-1, 0, "A"): (
        ("z+", 1, (-1, 1, "A")),
        ("z-", 1, (-1, -1, "A")),
    ),
    (1, 0, "B"): (
        ("y+", 1, (2, 0, "B0")),
    ),
    (-1, 0, "B"): (
        ("y-", 1, (2, 0, "B1")),
    ),
    (0, 1, "B"): (
        ("y+", 1, (1, 1, "B")),
        ("y-", 1, (-1, 1, "B")),
    ),
    (0, -1, "B"): (
        ("y+", 1, (1, -1, "B")),
        ("y-", 1, (-1, -1, "B")),
    ),
    (0, 2, "B"): (
        ("z+", 1, (0, 3, "B")),
        ("y+", 1, (1, 2, "B")),
        ("y-", 1, (-1, 2, "B")),
    ),
    (0, -2, "B"): (
        ("z-", 1, (0, -3, "B")),
        ("y+", 1, (1, -2, "B")),
        ("y-", 1, (-1, -2, "B")),
    ),
    (0, 2, "A"): (
        ("z+", 2, (0, 4, "A0")),
        ("z+", 1, (0, 3, "A")),
    ),
    (0, -2, "A"): (
        ("z-", 2, (0, 4, "A1")),
        ("z-", 1, (0, -3, "A")),
    ),
    (1, 1, "A"): (
        ("z+", 1, (1, 2, "A")),
    ),
    (1, -1, "A"): (
        ("z-", 1, (1, -2, "A")),
    ),
    (2, 0, "A"): (
        ("z+", 1, (2, 1, "A")),
        ("z-", 1, (2, -1, "A")),
    ),
    (-1, 1, "A"): (
        ("z+", 1, (-1, 2, "A")),
    ),
    (-1, -1, "A"): (
        ("z-", 1, (-1, -2, "A")),
    ),
    (0, 3, "B"): (
        ("z+", 1, (0, 4, "B0")),
        ("y+", 1, (1, 3, "B")),
        ("y-", 1, (-1, 3, "B")),
    ),
    (1, 1, "B"): (
        ("y+", 1, (2, 1, "B0")),
    ),
    (-1, 1, "B"): (
        ("y-", 1, (2, 1, "B1")),
    ),
    (0, -3, "B"): (
        ("z-", 1, (0, 4, "B1")),
        ("y+", 1, (1, -3, "B")),
        ("y-", 1, (-1, -3, "B")),
    ),
    (1, -1, "B"): (
        ("y+", 1, (2, -1, "B0")),
    ),
    (-1, -1, "B"): (
        ("y-", 1, (2, -1, "B1")),
    ),
    (1, 2, "A"): (
        ("z+", 2, (1, 4, "A0")),
        ("z+", 1, (1, 3, "A")),
    ),
    (1, -2, "A"): (
        ("z-", 2, (1, 4, "A1")),
        ("z-", 1, (1, -3, "A")),
    ),
    (1, 2, "B"): (
        ("y+", 1, (2, 2, "B0")),
    ),
    (-1, 2, "B"): (
        ("y-", 1, (2, 2, "B1")),
    ),
    (2, -1, "A"): (
        ("z-", 1, (2, -2, "A")),
    ),
    (2, 1, "A"): (
        ("z+", 1, (2, 2, "A")),
    ),
    (-1, 2, "A"): (
        ("z+", 2, (-1, 4, "A0")),
        ("z+", 1, (-1, 3, "A")),
    ),
    (1, -2, "B"): (
        ("y+", 1, (2, -2, "B0")),
    ),
    (-1, -2, "B"): (
        ("y-", 1, (2, -2, "B1")),
    ),
    (-1, -2, "A"): (
        ("z-", 2, (-1, 4, "A1")),
        ("z-", 1, (-1, -3, "A")),
    ),
    (0, 4, "B"): (
        ("y+", 2, (2, 4, "B0")),
        ("y-", 2, (2, 4, "B1")),
        ("y+", 1, (1, 4, "B")),
        ("y-", 1, (-1, 4, "B")),
    ),
    (1, 3, "B"): (
        ("y+", 1, (2, 3, "B0")),
    ),
    (-1, 3, "B"): (
        ("y-", 1, (2, 3, "B1")),
    ),
    (2, -2, "A"): (
        ("z-", 2, (2, 4, "A1")),
        ("z-", 1, (2, -3, "A")),
    ),
    (2, 2, "A"): (
        ("z+", 2, (2, 4, "A0")),
        ("z+", 1, (2, 3, "A")),
    ),
    (1, -3, "B"): (
        ("y+", 1, (2, -3, "B0")),
    ),
    (-1, -3, "B"): (
        ("y-", 1, (2, -3, "B1")),
    ),
}

FIRST_WORK = 50
STEPS = (
    (((0, 1, "A"),), 0),
    (((0, -1, "A"),), 0),
    (((1, 0, "A"),), 0),
    (((-1, 0, "A"),), 0),
    (((1, 0, "B"),), 0),
    (((-1, 0, "B"),), 0),
    (((0, 1, "B"),), 0),
    (((0, -1, "B"),), 0),
    (((0, 2, "B"),), 0),
    (((0, -2, "B"),), 0),
    (((0, 2, "A"),), 0),
    (((0, -2, "A"),), 0),
    (((1, 1, "A"),), 0),
    (((1, -1, "A"),), 0),
    (((2, 0, "A0"), (2, 0, "A1")), 0),
    (((-1, 1, "A"),), 0),
    (((-1, -1, "A"),), 1),
    (((2, 0, "B0"), (2, 0, "B1")), 7),
    (((0, 3, "B"),), 0),
    (((1, 1, "B"),), 0),
    (((-1, 1, "B"),), 0),
    (((0, -3, "B"),), 3),
    (((0, 3, "A"),), 0),
    (((1, -1, "B"),), 0),
    (((0, -3, "A"),), 0),
    (((-1, -1, "B"),), 2),
    (((1, 2, "A"),), 0),
    (((1, -2, "A"),), 2),
    (((1, 2, "B"),), 0),
    (((-1, 2, "B"),), 0),
    (((2, -1, "A"),), 0),
    (((2, 1, "A"),), 1),
    (((0, 4, "A0"), (0, 4, "A1")), 3),
    (((-1, 2, "A"),), 0),
    (((1, -2, "B"),), 0),
    (((-1, -2, "B"),), 0),
    (((-1, -2, "A"),), 0),
    (((0, 4, "B0"), (0, 4, "B1")), 0),
    (((1, 3, "B"),), 0),
    (((-1, 3, "B"),), 0),
    (((2, 1, "B0"), (2, 1, "B1")), 0),
    (((1, 3, "A"),), 0),
    (((1, -3, "A"),), 0),
    (((2, -2, "A"),), 0),
    (((2, 2, "A"),), 0),
    (((1, -3, "B"),), 0),
    (((-1, -3, "B"),), 0),
    (((1, 4, "A0"), (1, 4, "A1")), 0),
    (((2, -1, "B0"), (2, -1, "B1")), 0),
    (((-1, 3, "A"),), 0),
    (((-1, -3, "A"),), 0),
    (((2, 2, "B0"), (2, 2, "B1")), 0),
    (((-1, 4, "A0"), (-1, 4, "A1")), 0),
    (((2, -2, "B0"), (2, -2, "B1")), 0),
    (((2, -3, "A"),), 0),
    (((1, 4, "B"),), 0),
    (((-1, 4, "B"),), 0),
    (((2, 3, "A"),), 0),
    (((2, 4, "A0"), (2, 4, "A1")), 0),
    (((2, 3, "B0"), (2, 3, "B1")), 0),
    (((2, 4, "B0"), (2, 4, "B1")), 0),
    (((2, -3, "B0"), (2, -3, "B1")), 0),
)
MESSAGES = tuple(m for step, _ in STEPS for m in step)
REACH = tuple(sorted({(d[0], h * (1 if d[1] == "+" else -1) % (NY if d[0] == "y" else NZ)) for out in ROUTES.values() for d, h, _ in out}))
NUMBER = {m: i for i, m in enumerate(MESSAGES)}


def dot_nn(a, b):
    return lax.dot_general(a, b, (((1,), (0,)), ((), ())), preferred_element_type=F32)


def dot_nt(a, b):
    return lax.dot_general(a, b, (((1,), (1,)), ((), ())), preferred_element_type=F32)


def kernel(
    ch_hbm, cnt_hbm, basis_hbm, transfer_hbm, lc_hbm, lp_hbm, nb_hbm, pc_hbm, pp_hbm,
    out_ref,
    ch, basis, transfer, lc, nb, pc, cnt, lp, pp,
    live, win, row, cpl, bdiag, near, far, held, coefs,
    in_sem, recv_sem, send_sem, rim_recv, rim_send,
):
    gx = lax.axis_index("gx")
    gy = lax.axis_index("gy")
    z = gy // NY
    y = gy % NY
    dev = gx * NGY + gy
    total = NGX * NGY
    prv = (dev + total - 1) % total
    nxt = (dev + 1) % total
    prv_id = (prv // NGY, prv % NGY)
    nxt_id = (nxt // NGY, nxt % NGY)

    def reach(axis, steps):
        if axis == "y":
            return gx, z * NY + (y + steps) % NY
        return gx, ((z + steps) % NZ) * NY + y


    loads = [
        pltpu.make_async_copy(s, d, in_sem.at[i])
        for i, (s, d) in enumerate(
            [
                (ch_hbm, ch), (cnt_hbm, cnt), (basis_hbm, basis), (transfer_hbm, transfer),
                (nb_hbm, nb), (lp_hbm, lp), (pp_hbm, pp), (pc_hbm, pc), (lc_hbm, lc),
            ]
        )
    ]
    for load in loads:
        load.start()

    barrier = pltpu.get_barrier_semaphore()
    greeted = [reach(axis, steps) for axis, steps in REACH] + [prv_id, nxt_id]
    for d in greeted:
        pl.semaphore_signal(barrier, inc=1, device_id=d, device_id_type=MESH)

    mine, before, after = ((d % WIN) * QD for d in (dev, prv, nxt))

    lane = lax.broadcasted_iota(jnp.int32, (R, 128), 1)
    low = lane < 64

    def masks(q):
        return lane < cnt[2 * q], (lane >= 64) & (lane < cnt[2 * q + 1] + 64)

    def swap(tile):
        return jnp.concatenate([tile[:, 64:], tile[:, :64]], axis=1)

    for load in loads[:4]:
        load.wait()

    zero = jnp.zeros((R, 128), BF)
    parents = []
    for q in range(QD):
        m0, m1 = masks(q)
        tile = ch[:, 128 * q : 128 * q + 128]
        l0 = jnp.where(m0, tile, zero)
        l1 = jnp.where(m1, tile, zero)
        live[q + 1] = l0 + l1
        coef = dot_nn(jnp.concatenate([l0, l1], axis=0), basis[2 * q : 2 * q + 2].reshape(128, 64))
        coef = coef.astype(BF)
        pair = jnp.concatenate([coef[:R], coef[R:]], axis=1)
        win[0, mine + q] = pair
        win[1, mine + q] = jnp.concatenate([coef[R:], coef[:R]], axis=1)
        parents.append(dot_nn(pair, transfer[2 * q : 2 * q + 2].reshape(128, 64)).astype(BF))
        if q % 2:
            a, b = parents[q - 1], parents[q]
            at = pl.ds(gy * UD + q - 1, 2)
            row[0, at] = jnp.concatenate([a, b], axis=1).reshape(2, 16, 128)
            row[1, at] = jnp.concatenate([b, a], axis=1).reshape(2, 16, 128)

    pl.semaphore_wait(barrier, len(greeted))

    def rows_of(dy, dz, part):
        start, size = SPAN[part]
        origin = ((z + (NZ - dz)) % NZ) * NY + (y + (NY - dy)) % NY
        return pl.ds(origin * UD + start, size)

    def copy_of(rows, m, to):
        ref = row.at[0, rows]
        return pltpu.make_async_remote_copy(
            src_ref=ref, dst_ref=ref, send_sem=send_sem, recv_sem=recv_sem.at[NUMBER[m]],
            device_id=to, device_id_type=MESH,
        )

    def send_on(dy, dz, part):
        for d, steps, m in ROUTES.get((dy, dz, part), ()):
            steps = steps if d[1] == "+" else (NY if d[0] == "y" else NZ) - steps
            copy_of(rows_of(dy, dz, m[2]), m, reach(d[0], steps)).start()

    def receive(m):
        copy_of(rows_of(*m), m, greeted[0]).wait_recv()

    send_on(0, 0, "A")
    send_on(0, 0, "B")

    own = win.at[0, pl.ds(mine, QD)]
    rims = [
        pltpu.make_async_remote_copy(
            src_ref=s, dst_ref=d, send_sem=rim_send.at[i], recv_sem=rim_recv.at[i],
            device_id=to, device_id_type=MESH,
        )
        for i, (s, d, to) in enumerate(
            [
                (own, own, nxt_id),
                (own, own, prv_id),
                (live.at[pl.ds(QD, 1)], live.at[pl.ds(0, 1)], nxt_id),
                (live.at[pl.ds(1, 1)], live.at[pl.ds(QD + 1, 1)], prv_id),
            ]
        )
    ]
    for rim in rims:
        rim.start()

    def do_diag(q):
        b0, b1 = basis[2 * q], basis[2 * q + 1]
        o = jnp.zeros((64, 64), BF)
        bdiag[q, :64] = jnp.concatenate([b0, o], axis=1)
        bdiag[q, 64:] = jnp.concatenate([o, b1], axis=1)

    def do_near(q):
        o = jnp.zeros((64, 64), BF)
        o2 = jnp.zeros((64, 128), BF)
        top = jnp.concatenate([o, nb[2 * q, 0], nb[2 * q, 1], nb[2 * q, 2], o2], axis=1)
        low_rows = jnp.concatenate(
            [o2, nb[2 * q + 1, 0], nb[2 * q + 1, 1], nb[2 * q + 1, 2], o], axis=1
        )
        lhs = jnp.concatenate([live[q], live[q + 1], live[q + 2]], axis=1)
        near[q] = dot_nt(lhs, jnp.concatenate([top, low_rows], axis=0))

    def do_couple(q):
        for i in range(8):
            cpl[q, :, 128 * i : 128 * i + 128] = jnp.concatenate(
                [pc[q, 2 * i], pc[q, 2 * i + 1]], axis=1
            )

    def pick_leaves(p, q):
        a = win[p & 1, (p >> 1) & (WIN * QD - 1)]
        b = win[1 - (q & 1), (q >> 1) & (WIN * QD - 1)]
        return jnp.where(low, a, b)

    def pick_parents(p, q):
        a = (p >> 1) & (ROW_UNITS // 2 - 1)
        b = (q >> 1) & (ROW_UNITS // 2 - 1)
        return jnp.concatenate(
            [
                jnp.where(low[:16], row[p & 1, 2 * a + i], row[1 - (q & 1), 2 * b + i])
                for i in range(2)
            ],
            axis=0,
        )

    def leaf_sum(g):
        lhs = jnp.concatenate(
            [pick_leaves(lp[2 * i, g], lp[2 * i + 1, g]) for i in range(8)], axis=1
        )
        rhs = jnp.concatenate([lc[g, j] for j in range(16)], axis=1)
        return dot_nt(lhs, rhs)

    def do_far(q):
        far[q] = jnp.concatenate([leaf_sum(2 * q), leaf_sum(2 * q + 1)], axis=1)

    def take_rims():
        for rim in rims:
            rim.wait_recv()
        live[0] = jnp.where(dev > 0, live[0], zero)
        live[QD + 1] = jnp.where(dev < total - 1, live[QD + 1], zero)

        @pl.loop(0, QD)
        def _(t):
            win[1, before + t] = swap(win[0, before + t])
            win[1, after + t] = swap(win[0, after + t])

    def wait_load(i):
        return loads[i].wait

    work = [lambda q=q: do_diag(q) for q in range(QD)]
    work += [wait_load(4)] + [lambda q=q: do_near(q) for q in range(1, QD - 1)]
    work += [wait_load(7)] + [lambda q=q: do_couple(q) for q in range(QD)]
    work += [wait_load(5), wait_load(8), take_rims]
    work += [lambda: do_near(0), lambda: do_near(QD - 1)]
    work += [lambda q=q: do_far(q) for q in range(QD)]
    todo = iter(work)

    def do_work(n):
        for _ in range(n):
            next(todo, lambda: None)()

    do_work(FIRST_WORK)
    for step, pieces in STEPS:
        for m in step:
            receive(m)
        dy, dz, part = step[0]
        send_on(dy, dz, part[0] if len(step) == 2 else part)
        for m in step:
            rows = rows_of(*m)
            n = SPAN[m[2]][1]
            row[1, rows] = swap(row[0, rows].reshape(n * 16, 128)).reshape(n, 16, 128)
        do_work(pieces)
    for unit in todo:
        unit()

    loads[6].wait()
    for q in range(QD):
        lhs = jnp.concatenate(
            [pick_parents(pp[q, 2 * i], pp[q, 2 * i + 1]) for i in range(8)], axis=1
        )
        held[q] = dot_nt(lhs, cpl[q]).astype(BF)
    for q in range(QD):
        local = dot_nt(held[q], transfer[2 * q : 2 * q + 2].reshape(128, 64)) + far[q]
        coefs[q] = local.astype(BF)
    for q in range(QD):
        total_q = dot_nt(coefs[q], bdiag[q]) + near[q]
        m0, m1 = masks(q)
        out_ref[:, 128 * q : 128 * q + 128] = jnp.where(m0 | m1, total_q, 0.0).astype(BF)

    for rim in rims:
        rim.wait_send()
    copy_of(pl.ds(0, ROW_UNITS - UD), MESSAGES[0], greeted[0]).wait_send()


def per_device(
    charges, panel_counts, basis, transfer, leaf_coupling, leaf_partners, near_blocks,
    parent_coupling, parent_partners,
):
    n = charges.shape[0]
    result = pl.pallas_call(
        kernel,
        out_shape=jax.ShapeDtypeStruct((R, n), BF),
        in_specs=[pl.BlockSpec(memory_space=pltpu.HBM)] * 9,
        out_specs=pl.BlockSpec(memory_space=pltpu.VMEM),
        scratch_shapes=[
            pltpu.VMEM((R, n), BF),
            pltpu.VMEM(basis.shape, BF),
            pltpu.VMEM(transfer.shape, BF),
            pltpu.VMEM(leaf_coupling.shape, BF),
            pltpu.VMEM(near_blocks.shape, BF),
            pltpu.VMEM(parent_coupling.shape, BF),
            pltpu.SMEM((LD,), jnp.int32),
            pltpu.SMEM((16, LD), jnp.int32),
            pltpu.SMEM((QD, 16), jnp.int32),
            pltpu.VMEM((QD + 2, R, 128), BF),
            pltpu.VMEM((2, WIN * QD, R, 128), BF),
            pltpu.VMEM((2, ROW_UNITS, 16, 128), BF),
            pltpu.VMEM((QD, 64, 1024), BF),
            pltpu.VMEM((QD, 128, 128), BF),
            pltpu.VMEM((QD, R, 128), F32),
            pltpu.VMEM((QD, R, 128), F32),
            pltpu.VMEM((QD, R, 64), BF),
            pltpu.VMEM((QD, R, 128), BF),
            pltpu.SemaphoreType.DMA((9,)),
            pltpu.SemaphoreType.DMA((len(MESSAGES),)),
            pltpu.SemaphoreType.DMA,
            pltpu.SemaphoreType.DMA((4,)),
            pltpu.SemaphoreType.DMA((4,)),
        ],
        compiler_params=pltpu.CompilerParams(
            collective_id=0, has_side_effects=True, vmem_limit_bytes=56 * 1024 * 1024
        ),
    )(
        charges.T, panel_counts, basis, transfer, leaf_coupling, leaf_partners.T, near_blocks,
        parent_coupling, parent_partners,
    )
    return result.T


def solution(mesh):
    in_specs = (
        P(("gx", "gy"), None),
        P(("gx", "gy")),
        P(("gx", "gy"), None, None),
        P(("gx", "gy"), None, None),
        P(("gx", "gy"), None, None, None),
        P(("gx", "gy"), None),
        P(("gx", "gy"), None, None, None),
        P(("gx", "gy"), None, None, None),
        P(("gx", "gy"), None),
    )
    out_specs = P(("gx", "gy"), None)
    return jax.shard_map(
        per_device, mesh=mesh, in_specs=in_specs, out_specs=out_specs, check_vma=False
    )
```

```python
import jax
import jax.numpy as jnp
from jax import lax
from jax.experimental import pallas as pl
from jax.experimental.pallas import tpu as pltpu
from jax.sharding import PartitionSpec as P

BF = jnp.bfloat16
F32 = jnp.float32
MESH = pl.DeviceIdType.MESH

NY = 4
NZ = 8
NGX = 8
NGY = NY * NZ
LD = 32
QD = 16
UD = QD
ROW_UNITS = NGY * UD
R = 32
WIN = 4
RIM = 4

SPAN = {"A": (0, 7), "A0": (0, 4), "A1": (4, 3), "B": (7, 9), "B0": (7, 5), "B1": (12, 4)}

FIRST = (
    ("z+", 2, (0, 2, "B")),
    ("y+", 1, (1, 0, "B")),
    ("y+", 2, (2, 0, "A0")),
    ("z-", 2, (0, -2, "B")),
    ("y-", 2, (2, 0, "A1")),
    ("z-", 1, (0, -1, "B")),
    ("z+", 1, (0, 1, "B")),
    ("y-", 1, (-1, 0, "A")),
    ("y-", 1, (-1, 0, "B")),
    ("z+", 1, (0, 1, "A")),
    ("z-", 1, (0, -1, "A")),
    ("y+", 1, (1, 0, "A")),
)

ROUTES = {
    (1, 0, "B"): (("y+", 1, (2, 0, "B0")),),
    (-1, 0, "A"): (("z+", 1, (-1, 1, "A")), ("z-", 1, (-1, -1, "A"))),
    (0, 1, "B"): (("y+", 1, (1, 1, "B")), ("y-", 1, (-1, 1, "B"))),
    (0, -1, "B"): (("y+", 1, (1, -1, "B")), ("y-", 1, (-1, -1, "B"))),
    (1, 0, "A"): (("z+", 1, (1, 1, "A")), ("z-", 1, (1, -1, "A"))),
    (-1, 0, "B"): (("y-", 1, (2, 0, "B1")),),
    (0, 1, "A"): (("z+", 1, (0, 2, "A")),),
    (0, -1, "A"): (("z-", 1, (0, -2, "A")),),
    (0, 2, "B"): (("z+", 1, (0, 3, "B")), ("y+", 1, (1, 2, "B")), ("y-", 1, (-1, 2, "B"))),
    (0, -2, "B"): (("z-", 1, (0, -3, "B")), ("y+", 1, (1, -2, "B")), ("y-", 1, (-1, -2, "B"))),
    (2, 0, "A"): (("z+", 1, (2, 1, "A")), ("z-", 1, (2, -1, "A"))),
    (-1, 1, "A"): (("z+", 1, (-1, 2, "A")),),
    (-1, -1, "A"): (("z-", 1, (-1, -2, "A")),),
    (-1, 1, "B"): (("y-", 1, (2, 1, "B1")),),
    (1, 1, "B"): (("y+", 1, (2, 1, "B0")),),
    (1, 1, "A"): (("z+", 1, (1, 2, "A")),),
    (1, -1, "A"): (("z-", 1, (1, -2, "A")),),
    (0, 2, "A"): (("z+", 1, (0, 3, "A")),),
    (-1, -1, "B"): (("y-", 1, (2, -1, "B1")),),
    (1, -1, "B"): (("y+", 1, (2, -1, "B0")),),
    (0, -2, "A"): (("z-", 1, (0, -3, "A")),),
    (0, 3, "B"): (("z+", 1, (0, 4, "B0")), ("y+", 1, (1, 3, "B")), ("y-", 1, (-1, 3, "B"))),
    (1, 2, "B"): (("y+", 1, (2, 2, "B0")),),
    (0, -3, "B"): (("z-", 1, (0, 4, "B1")), ("y+", 1, (1, -3, "B")), ("y-", 1, (-1, -3, "B"))),
    (-1, 2, "B"): (("y-", 1, (2, 2, "B1")),),
    (2, 1, "A"): (("z+", 1, (2, 2, "A")),),
    (2, -1, "A"): (("z-", 1, (2, -2, "A")),),
    (1, -2, "B"): (("y+", 1, (2, -2, "B0")),),
    (-1, -2, "B"): (("y-", 1, (2, -2, "B1")),),
    (-1, 2, "A"): (("z+", 1, (-1, 3, "A")),),
    (-1, -2, "A"): (("z-", 1, (-1, -3, "A")),),
    (1, 2, "A"): (("z+", 1, (1, 3, "A")),),
    (1, -2, "A"): (("z-", 1, (1, -3, "A")),),
    (0, 3, "A"): (("z+", 1, (0, 4, "A0")),),
    (0, -3, "A"): (("z-", 1, (0, 4, "A1")),),
    (1, 3, "B"): (("y+", 1, (2, 3, "B0")),),
    (0, 4, "B"): (("y+", 2, (2, 4, "B0")), ("y-", 2, (2, 4, "B1")), ("y+", 1, (1, 4, "B")), ("y-", 1, (-1, 4, "B"))),
    (-1, 3, "B"): (("y-", 1, (2, 3, "B1")),),
    (2, 2, "A"): (("z+", 2, (2, 4, "A0")), ("z+", 1, (2, 3, "A"))),
    (2, -2, "A"): (("z-", 2, (2, 4, "A1")), ("z-", 1, (2, -3, "A"))),
    (-1, 3, "A"): (("z+", 1, (-1, 4, "A0")),),
    (-1, -3, "A"): (("z-", 1, (-1, 4, "A1")),),
    (-1, -3, "B"): (("y-", 1, (2, -3, "B1")),),
    (1, -3, "B"): (("y+", 1, (2, -3, "B0")),),
    (1, 3, "A"): (("z+", 1, (1, 4, "A0")),),
    (1, -3, "A"): (("z-", 1, (1, 4, "A1")),),
}

RIM_AT = (-1, -1, 12, 22)
FIRST_WORK = 50
STEPS = (
    (((1, 0, "B"),), 0),
    (((-1, 0, "A"),), 0),
    (((0, 1, "B"),), 0),
    (((0, -1, "B"),), 0),
    (((1, 0, "A"),), 0),
    (((-1, 0, "B"),), 0),
    (((0, 1, "A"),), 0),
    (((0, -1, "A"),), 0),
    (((0, 2, "B"),), 0),
    (((0, -2, "B"),), 0),
    (((2, 0, "A0"), (2, 0, "A1")), 0),
    (((-1, 1, "A"),), 0),
    (((-1, -1, "A"),), 0),
    (((-1, 1, "B"),), 0),
    (((1, 1, "B"),), 0),
    (((1, 1, "A"),), 0),
    (((1, -1, "A"),), 0),
    (((0, 2, "A"),), 0),
    (((-1, -1, "B"),), 0),
    (((1, -1, "B"),), 0),
    (((0, -2, "A"),), 0),
    (((2, 0, "B0"), (2, 0, "B1")), 0),
    (((0, 3, "B"),), 0),
    (((1, 2, "B"),), 0),
    (((0, -3, "B"),), 0),
    (((-1, 2, "B"),), 0),
    (((2, 1, "A"),), 0),
    (((2, -1, "A"),), 0),
    (((1, -2, "B"),), 0),
    (((-1, -2, "B"),), 0),
    (((-1, 2, "A"),), 0),
    (((-1, -2, "A"),), 0),
    (((1, 2, "A"),), 0),
    (((1, -2, "A"),), 0),
    (((2, 1, "B0"), (2, 1, "B1")), 0),
    (((2, -1, "B0"), (2, -1, "B1")), 0),
    (((0, 3, "A"),), 0),
    (((0, -3, "A"),), 0),
    (((1, 3, "B"),), 0),
    (((0, 4, "B0"), (0, 4, "B1")), 0),
    (((-1, 3, "B"),), 0),
    (((2, 2, "A"),), 0),
    (((2, -2, "A"),), 8),
    (((-1, 3, "A"),), 0),
    (((-1, -3, "A"),), 0),
    (((-1, -3, "B"),), 0),
    (((1, -3, "B"),), 0),
    (((2, 2, "B0"), (2, 2, "B1")), 1),
    (((1, 3, "A"),), 0),
    (((1, -3, "A"),), 0),
    (((2, -2, "B0"), (2, -2, "B1")), 1),
    (((0, 4, "A0"), (0, 4, "A1")), 9),
    (((-1, 4, "B"),), 0),
    (((2, 3, "A"),), 0),
    (((2, -3, "A"),), 0),
    (((2, 3, "B0"), (2, 3, "B1")), 0),
    (((1, 4, "B"),), 0),
    (((2, 4, "A0"), (2, 4, "A1")), 0),
    (((2, 4, "B0"), (2, 4, "B1")), 0),
    (((-1, 4, "A0"), (-1, 4, "A1")), 0),
    (((2, -3, "B0"), (2, -3, "B1")), 0),
    (((1, 4, "A0"), (1, 4, "A1")), 0),
)

MESSAGES = tuple(m for step, _ in STEPS for m in step)
REACH = tuple(sorted({(d[0], h * (1 if d[1] == "+" else -1) % (NY if d[0] == "y" else NZ)) for out in (FIRST, *ROUTES.values()) for d, h, _ in out}))
NUMBER = {m: i for i, m in enumerate(MESSAGES)}


def dot_nn(a, b):
    return lax.dot_general(a, b, (((1,), (0,)), ((), ())), preferred_element_type=F32)


def dot_nt(a, b):
    return lax.dot_general(a, b, (((1,), (1,)), ((), ())), preferred_element_type=F32)


def kernel(
    ch_hbm, cnt_hbm, basis_hbm, transfer_hbm, lc_hbm, lp_hbm, nb_hbm, pc_hbm, pp_hbm,
    out_ref,
    ch, basis, transfer, lc, nb, pc, cnt, lp, pp,
    live, win, row, cpl, bdiag, near, far, held, coefs,
    in_sem, recv_sem, send_sem, rim_recv, rim_send,
):
    gx = lax.axis_index("gx")
    gy = lax.axis_index("gy")
    z = gy // NY
    y = gy % NY
    dev = gx * NGY + gy
    total = NGX * NGY
    prv = (dev + total - 1) % total
    nxt = (dev + 1) % total
    prv_id = (prv // NGY, prv % NGY)
    nxt_id = (nxt // NGY, nxt % NGY)

    def reach(axis, steps):
        if axis == "y":
            return gx, z * NY + (y + steps) % NY
        return gx, ((z + steps) % NZ) * NY + y


    loads = [
        pltpu.make_async_copy(s, d, in_sem.at[i])
        for i, (s, d) in enumerate(
            [
                (ch_hbm, ch), (cnt_hbm, cnt), (basis_hbm, basis), (transfer_hbm, transfer),
                (nb_hbm, nb), (lp_hbm, lp), (pp_hbm, pp), (pc_hbm, pc), (lc_hbm, lc),
            ]
        )
    ]
    for load in loads:
        load.start()

    barrier = pltpu.get_barrier_semaphore()
    greeted = [reach(axis, steps) for axis, steps in REACH] + [prv_id, nxt_id]
    for d in greeted:
        pl.semaphore_signal(barrier, inc=1, device_id=d, device_id_type=MESH)

    mine, before, after = ((d % WIN) * QD for d in (dev, prv, nxt))

    lane = lax.broadcasted_iota(jnp.int32, (R, 128), 1)
    low = lane < 64

    def masks(q):
        return lane < cnt[2 * q], (lane >= 64) & (lane < cnt[2 * q + 1] + 64)

    def swap(tile):
        return jnp.concatenate([tile[:, 64:], tile[:, :64]], axis=1)

    for load in loads[:4]:
        load.wait()

    zero = jnp.zeros((R, 128), BF)
    parents = []
    for q in range(QD):
        m0, m1 = masks(q)
        tile = ch[:, 128 * q : 128 * q + 128]
        l0 = jnp.where(m0, tile, zero)
        l1 = jnp.where(m1, tile, zero)
        live[q + 1] = l0 + l1
        coef = dot_nn(jnp.concatenate([l0, l1], axis=0), basis[2 * q : 2 * q + 2].reshape(128, 64))
        coef = coef.astype(BF)
        pair = jnp.concatenate([coef[:R], coef[R:]], axis=1)
        win[0, mine + q] = pair
        win[1, mine + q] = jnp.concatenate([coef[R:], coef[:R]], axis=1)
        parents.append(dot_nn(pair, transfer[2 * q : 2 * q + 2].reshape(128, 64)).astype(BF))
        if q % 2:
            a, b = parents[q - 1], parents[q]
            at = pl.ds(gy * UD + q - 1, 2)
            row[0, at] = jnp.concatenate([a, b], axis=1).reshape(2, 16, 128)
            row[1, at] = jnp.concatenate([b, a], axis=1).reshape(2, 16, 128)

    pl.semaphore_wait(barrier, len(greeted))

    def rows_of(dy, dz, part):
        start, size = SPAN[part]
        origin = ((z + (NZ - dz)) % NZ) * NY + (y + (NY - dy)) % NY
        return pl.ds(origin * UD + start, size)

    def copy_of(rows, m, to):
        ref = row.at[0, rows]
        return pltpu.make_async_remote_copy(
            src_ref=ref, dst_ref=ref, send_sem=send_sem, recv_sem=recv_sem.at[NUMBER[m]],
            device_id=to, device_id_type=MESH,
        )

    def send_on(dy, dz, part):
        for d, steps, m in ROUTES.get((dy, dz, part), ()):
            steps = steps if d[1] == "+" else (NY if d[0] == "y" else NZ) - steps
            copy_of(rows_of(dy, dz, m[2]), m, reach(d[0], steps)).start()

    def receive(m):
        copy_of(rows_of(*m), m, greeted[0]).wait_recv()

    for d, steps, m in FIRST:
        steps = steps if d[1] == "+" else (NY if d[0] == "y" else NZ) - steps
        copy_of(rows_of(0, 0, m[2]), m, reach(d[0], steps)).start()

    def rim_part(i):
        return win.at[0, pl.ds(mine + i * RIM, RIM)]

    rims = [
        pltpu.make_async_remote_copy(
            src_ref=s, dst_ref=d, send_sem=rim_send.at[i], recv_sem=rim_recv.at[i],
            device_id=to, device_id_type=MESH,
        )
        for i, (s, d, to) in enumerate(
            [
                (live.at[pl.ds(QD, 1)], live.at[pl.ds(0, 1)], nxt_id),
                (live.at[pl.ds(1, 1)], live.at[pl.ds(QD + 1, 1)], prv_id),
            ]
            + [
                (rim_part(j), rim_part(j), to)
                for j in range(QD // RIM)
                for to in (nxt_id, prv_id)
            ]
        )
    ]
    def start_rims(step):
        for j, at in enumerate(RIM_AT):
            if at == step:
                for rim in rims[2 + 2 * j : 4 + 2 * j] + (rims[:2] if j == 0 else []):
                    rim.start()

    start_rims(-1)

    def do_diag(q):
        b0, b1 = basis[2 * q], basis[2 * q + 1]
        o = jnp.zeros((64, 64), BF)
        both = [jnp.concatenate([b0, o], axis=1), jnp.concatenate([o, b1], axis=1)]
        bdiag[q] = jnp.concatenate(both, axis=0).T

    def do_near(q):
        o = jnp.zeros((64, 64), BF)
        o2 = jnp.zeros((64, 128), BF)
        top = jnp.concatenate([o, nb[2 * q, 0], nb[2 * q, 1], nb[2 * q, 2], o2], axis=1)
        low_rows = jnp.concatenate(
            [o2, nb[2 * q + 1, 0], nb[2 * q + 1, 1], nb[2 * q + 1, 2], o], axis=1
        )
        lhs = jnp.concatenate([live[q], live[q + 1], live[q + 2]], axis=1)
        near[q] = dot_nt(lhs, jnp.concatenate([top, low_rows], axis=0))

    def do_couple(q):
        for i in range(8):
            cpl[q, :, 128 * i : 128 * i + 128] = jnp.concatenate(
                [pc[q, 2 * i], pc[q, 2 * i + 1]], axis=1
            )

    def pick_leaves(p, q):
        a = win[p & 1, (p >> 1) & (WIN * QD - 1)]
        b = win[1 - (q & 1), (q >> 1) & (WIN * QD - 1)]
        return jnp.where(low, a, b)

    def pick_parents(p, q):
        a = (p >> 1) & (ROW_UNITS // 2 - 1)
        b = (q >> 1) & (ROW_UNITS // 2 - 1)
        return jnp.concatenate(
            [
                jnp.where(low[:16], row[p & 1, 2 * a + i], row[1 - (q & 1), 2 * b + i])
                for i in range(2)
            ],
            axis=0,
        )

    def leaf_sum(g):
        lhs = jnp.concatenate(
            [pick_leaves(lp[2 * i, g], lp[2 * i + 1, g]) for i in range(8)], axis=1
        )
        rhs = jnp.concatenate([lc[g, j] for j in range(16)], axis=1)
        return dot_nt(lhs, rhs)

    def do_far(q):
        far[q] = jnp.concatenate([leaf_sum(2 * q), leaf_sum(2 * q + 1)], axis=1)

    def take_rims():
        for rim in rims:
            rim.wait_recv()
        live[0] = jnp.where(dev > 0, live[0], zero)
        live[QD + 1] = jnp.where(dev < total - 1, live[QD + 1], zero)

        @pl.loop(0, QD)
        def _(t):
            win[1, before + t] = swap(win[0, before + t])
            win[1, after + t] = swap(win[0, after + t])

    def wait_load(i):
        return loads[i].wait

    work = [lambda q=q: do_diag(q) for q in range(QD)]
    work += [wait_load(4)] + [lambda q=q: do_near(q) for q in range(1, QD - 1)]
    work += [wait_load(7)] + [lambda q=q: do_couple(q) for q in range(QD)]
    work += [wait_load(5), wait_load(8), take_rims]
    work += [lambda: do_near(0), lambda: do_near(QD - 1)]
    work += [lambda q=q: do_far(q) for q in range(QD)]
    todo = iter(work)

    def do_work(n):
        for _ in range(n):
            next(todo, lambda: None)()

    do_work(FIRST_WORK)
    for number, (step, pieces) in enumerate(STEPS):
        for m in step:
            receive(m)
        dy, dz, part = step[0]
        send_on(dy, dz, part[0] if len(step) == 2 else part)
        start_rims(number)
        for m in step:
            rows = rows_of(*m)
            n = SPAN[m[2]][1]
            row[1, rows] = swap(row[0, rows].reshape(n * 16, 128)).reshape(n, 16, 128)
        do_work(pieces)
    for unit in todo:
        unit()

    loads[6].wait()
    for q in range(QD):
        lhs = jnp.concatenate(
            [pick_parents(pp[q, 2 * i], pp[q, 2 * i + 1]) for i in range(8)], axis=1
        )
        held[q] = dot_nt(lhs, cpl[q]).astype(BF)
    for q in range(QD):
        local = dot_nt(held[q], transfer[2 * q : 2 * q + 2].reshape(128, 64)) + far[q]
        coefs[q] = local.astype(BF)
    for q in range(QD):
        total_q = dot_nn(coefs[q], bdiag[q]) + near[q]
        m0, m1 = masks(q)
        out_ref[:, 128 * q : 128 * q + 128] = jnp.where(m0 | m1, total_q, 0.0).astype(BF)

    for rim in rims:
        rim.wait_send()
    copy_of(pl.ds(0, ROW_UNITS - UD), MESSAGES[0], greeted[0]).wait_send()


def per_device(
    charges, panel_counts, basis, transfer, leaf_coupling, leaf_partners, near_blocks,
    parent_coupling, parent_partners,
):
    n = charges.shape[0]
    result = pl.pallas_call(
        kernel,
        out_shape=pltpu.VMEM((R, n), BF),
        in_specs=[pl.BlockSpec(memory_space=pltpu.HBM)] * 9,
        out_specs=pl.BlockSpec(memory_space=pltpu.VMEM),
        scratch_shapes=[
            pltpu.VMEM((R, n), BF),
            pltpu.VMEM(basis.shape, BF),
            pltpu.VMEM(transfer.shape, BF),
            pltpu.VMEM(leaf_coupling.shape, BF),
            pltpu.VMEM(near_blocks.shape, BF),
            pltpu.VMEM(parent_coupling.shape, BF),
            pltpu.SMEM((LD,), jnp.int32),
            pltpu.SMEM((16, LD), jnp.int32),
            pltpu.SMEM((QD, 16), jnp.int32),
            pltpu.VMEM((QD + 2, R, 128), BF),
            pltpu.VMEM((2, WIN * QD, R, 128), BF),
            pltpu.VMEM((2, ROW_UNITS, 16, 128), BF),
            pltpu.VMEM((QD, 64, 1024), BF),
            pltpu.VMEM((QD, 128, 128), BF),
            pltpu.VMEM((QD, R, 128), F32),
            pltpu.VMEM((QD, R, 128), F32),
            pltpu.VMEM((QD, R, 64), BF),
            pltpu.VMEM((QD, R, 128), BF),
            pltpu.SemaphoreType.DMA((9,)),
            pltpu.SemaphoreType.DMA((len(MESSAGES),)),
            pltpu.SemaphoreType.DMA,
            pltpu.SemaphoreType.DMA((2 + 2 * QD // RIM,)),
            pltpu.SemaphoreType.DMA((2 + 2 * QD // RIM,)),
        ],
        compiler_params=pltpu.CompilerParams(
            collective_id=0, has_side_effects=True, vmem_limit_bytes=56 * 1024 * 1024
        ),
    )(
        charges.T, panel_counts, basis, transfer, leaf_coupling, leaf_partners.T, near_blocks,
        parent_coupling, parent_partners,
    )
    return result.T


def solution(mesh):
    in_specs = (
        P(("gx", "gy"), None),
        P(("gx", "gy")),
        P(("gx", "gy"), None, None),
        P(("gx", "gy"), None, None),
        P(("gx", "gy"), None, None, None),
        P(("gx", "gy"), None),
        P(("gx", "gy"), None, None, None),
        P(("gx", "gy"), None, None, None),
        P(("gx", "gy"), None),
    )
    out_specs = P(("gx", "gy"), None)
    return jax.shard_map(
        per_device, mesh=mesh, in_specs=in_specs, out_specs=out_specs, check_vma=False
    )
```

```python
import jax
import jax.numpy as jnp
from jax import lax
from jax.experimental import pallas as pl
from jax.experimental.pallas import tpu as pltpu
from jax.sharding import PartitionSpec as P

BF = jnp.bfloat16
F32 = jnp.float32
MESH = pl.DeviceIdType.MESH

NY = 4
NZ = 8
NGX = 8
NGY = NY * NZ
LD = 32
QD = 16
UD = QD
ROW_UNITS = NGY * UD
R = 32
WIN = 4
RIM = 4

SPAN = {"A": (0, 7), "A0": (0, 4), "A1": (4, 3), "B": (7, 9), "B0": (7, 5), "B1": (12, 4)}

FIRST = (
    ("z+", 2, (0, 2, "B")),
    ("y+", 1, (1, 0, "B")),
    ("y+", 2, (2, 0, "A0")),
    ("z-", 2, (0, -2, "B")),
    ("y-", 2, (2, 0, "A1")),
    ("z-", 1, (0, -1, "B")),
    ("z+", 1, (0, 1, "B")),
    ("y-", 1, (-1, 0, "A")),
    ("y-", 1, (-1, 0, "B")),
    ("z+", 1, (0, 1, "A")),
    ("z-", 1, (0, -1, "A")),
    ("y+", 1, (1, 0, "A")),
)

ROUTES = {
    (1, 0, "B"): (("y+", 1, (2, 0, "B0")),),
    (-1, 0, "A"): (("z+", 1, (-1, 1, "A")), ("z-", 1, (-1, -1, "A"))),
    (0, 1, "B"): (("y+", 1, (1, 1, "B")), ("y-", 1, (-1, 1, "B"))),
    (0, -1, "B"): (("y+", 1, (1, -1, "B")), ("y-", 1, (-1, -1, "B"))),
    (1, 0, "A"): (("z+", 1, (1, 1, "A")), ("z-", 1, (1, -1, "A"))),
    (-1, 0, "B"): (("y-", 1, (2, 0, "B1")),),
    (0, 1, "A"): (("z+", 1, (0, 2, "A")),),
    (0, -1, "A"): (("z-", 1, (0, -2, "A")),),
    (0, 2, "B"): (("z+", 1, (0, 3, "B")), ("y+", 1, (1, 2, "B")), ("y-", 1, (-1, 2, "B"))),
    (0, -2, "B"): (("z-", 1, (0, -3, "B")), ("y+", 1, (1, -2, "B")), ("y-", 1, (-1, -2, "B"))),
    (2, 0, "A"): (("z+", 1, (2, 1, "A")), ("z-", 1, (2, -1, "A"))),
    (-1, 1, "A"): (("z+", 1, (-1, 2, "A")),),
    (-1, -1, "A"): (("z-", 1, (-1, -2, "A")),),
    (-1, 1, "B"): (("y-", 1, (2, 1, "B1")),),
    (1, 1, "B"): (("y+", 1, (2, 1, "B0")),),
    (1, 1, "A"): (("z+", 1, (1, 2, "A")),),
    (1, -1, "A"): (("z-", 1, (1, -2, "A")),),
    (0, 2, "A"): (("z+", 1, (0, 3, "A")),),
    (-1, -1, "B"): (("y-", 1, (2, -1, "B1")),),
    (1, -1, "B"): (("y+", 1, (2, -1, "B0")),),
    (0, -2, "A"): (("z-", 1, (0, -3, "A")),),
    (0, 3, "B"): (("z+", 1, (0, 4, "B0")), ("y+", 1, (1, 3, "B")), ("y-", 1, (-1, 3, "B"))),
    (1, 2, "B"): (("y+", 1, (2, 2, "B0")),),
    (0, -3, "B"): (("z-", 1, (0, 4, "B1")), ("y+", 1, (1, -3, "B")), ("y-", 1, (-1, -3, "B"))),
    (-1, 2, "B"): (("y-", 1, (2, 2, "B1")),),
    (2, 1, "A"): (("z+", 1, (2, 2, "A")),),
    (2, -1, "A"): (("z-", 1, (2, -2, "A")),),
    (1, -2, "B"): (("y+", 1, (2, -2, "B0")),),
    (-1, 2, "A"): (("z+", 1, (-1, 3, "A")),),
    (-1, -2, "A"): (("z-", 1, (-1, -3, "A")),),
    (-1, -2, "B"): (("y-", 1, (2, -2, "B1")),),
    (1, 2, "A"): (("z+", 1, (1, 3, "A")),),
    (1, -2, "A"): (("z-", 1, (1, -3, "A")),),
    (0, 3, "A"): (("z+", 1, (0, 4, "A0")),),
    (0, -3, "A"): (("z-", 1, (0, 4, "A1")),),
    (0, 4, "B"): (("y+", 2, (2, 4, "B0")), ("y-", 2, (2, 4, "B1")), ("y+", 1, (1, 4, "B")), ("y-", 1, (-1, 4, "B"))),
    (1, 3, "B"): (("y+", 1, (2, 3, "B0")),),
    (-1, 3, "B"): (("y-", 1, (2, 3, "B1")),),
    (2, 2, "A"): (("z+", 2, (2, 4, "A0")), ("z+", 1, (2, 3, "A"))),
    (2, -2, "A"): (("z-", 2, (2, 4, "A1")), ("z-", 1, (2, -3, "A"))),
    (-1, 3, "A"): (("z+", 1, (-1, 4, "A0")),),
    (-1, -3, "A"): (("z-", 1, (-1, 4, "A1")),),
    (-1, -3, "B"): (("y-", 1, (2, -3, "B1")),),
    (1, -3, "B"): (("y+", 1, (2, -3, "B0")),),
    (1, 3, "A"): (("z+", 1, (1, 4, "A0")),),
    (1, -3, "A"): (("z-", 1, (1, 4, "A1")),),
}

RIM_AT = (-1, -1, 8, 16)
FIRST_WORK = 50
STEPS = (
    (((1, 0, "B"),), 0),
    (((-1, 0, "A"),), 0),
    (((0, 1, "B"),), 0),
    (((0, -1, "B"),), 0),
    (((1, 0, "A"),), 0),
    (((-1, 0, "B"),), 0),
    (((0, 1, "A"),), 0),
    (((0, -1, "A"),), 0),
    (((0, 2, "B"),), 0),
    (((0, -2, "B"),), 0),
    (((2, 0, "A0"), (2, 0, "A1")), 0),
    (((-1, 1, "A"),), 0),
    (((-1, -1, "A"),), 0),
    (((-1, 1, "B"),), 0),
    (((1, 1, "B"),), 0),
    (((1, 1, "A"),), 0),
    (((1, -1, "A"),), 0),
    (((0, 2, "A"),), 0),
    (((-1, -1, "B"),), 0),
    (((1, -1, "B"),), 0),
    (((0, -2, "A"),), 0),
    (((2, 0, "B0"), (2, 0, "B1")), 0),
    (((0, 3, "B"),), 0),
    (((1, 2, "B"),), 0),
    (((0, -3, "B"),), 0),
    (((-1, 2, "B"),), 0),
    (((2, 1, "A"),), 0),
    (((2, -1, "A"),), 0),
    (((1, -2, "B"),), 0),
    (((-1, 2, "A"),), 0),
    (((-1, -2, "A"),), 0),
    (((-1, -2, "B"),), 0),
    (((1, 2, "A"),), 0),
    (((2, 1, "B0"), (2, 1, "B1")), 0),
    (((1, -2, "A"),), 0),
    (((0, 3, "A"),), 0),
    (((0, -3, "A"),), 0),
    (((2, -1, "B0"), (2, -1, "B1")), 0),
    (((0, 4, "B0"), (0, 4, "B1")), 0),
    (((1, 3, "B"),), 0),
    (((-1, 3, "B"),), 8),
    (((2, 2, "A"),), 0),
    (((2, -2, "A"),), 0),
    (((-1, 3, "A"),), 0),
    (((-1, -3, "A"),), 0),
    (((-1, -3, "B"),), 0),
    (((1, -3, "B"),), 0),
    (((2, 2, "B0"), (2, 2, "B1")), 2),
    (((1, 3, "A"),), 0),
    (((1, -3, "A"),), 0),
    (((2, -2, "B0"), (2, -2, "B1")), 0),
    (((0, 4, "A0"), (0, 4, "A1")), 9),
    (((-1, 4, "B"),), 0),
    (((1, 4, "B"),), 0),
    (((2, 3, "A"),), 0),
    (((2, -3, "A"),), 0),
    (((2, 3, "B0"), (2, 3, "B1")), 0),
    (((-1, 4, "A0"), (-1, 4, "A1")), 0),
    (((2, 4, "B0"), (2, 4, "B1")), 0),
    (((2, 4, "A0"), (2, 4, "A1")), 0),
    (((2, -3, "B0"), (2, -3, "B1")), 0),
    (((1, 4, "A0"), (1, 4, "A1")), 0),
)

RELAY_AT = 12
MESSAGES = tuple(m for step, _ in STEPS for m in step)
REACH = tuple(sorted({(d[0], h * (1 if d[1] == "+" else -1) % (NY if d[0] == "y" else NZ)) for out in (FIRST, *ROUTES.values()) for d, h, _ in out}))
NUMBER = {m: i for i, m in enumerate(MESSAGES)}


def dot_nn(a, b):
    return lax.dot_general(a, b, (((1,), (0,)), ((), ())), preferred_element_type=F32)


def dot_nt(a, b):
    return lax.dot_general(a, b, (((1,), (1,)), ((), ())), preferred_element_type=F32)


def kernel(
    ch_hbm, cnt_hbm, basis_hbm, transfer_hbm, lc_hbm, lp_hbm, nb_hbm, pc_hbm, pp_hbm,
    out_ref,
    ch, basis, transfer, lc, nb, pc, cnt, lp, pp,
    live, win, row, cpl, bdiag, near, far, held, coefs,
    relay, in_sem, recv_sem, send_sem, rim_recv, rim_send, relay_recv, relay_send,
):
    gx = lax.axis_index("gx")
    gy = lax.axis_index("gy")
    z = gy // NY
    y = gy % NY
    dev = gx * NGY + gy
    total = NGX * NGY
    prv = (dev + total - 1) % total
    nxt = (dev + 1) % total
    prv_id = (prv // NGY, prv % NGY)
    nxt_id = (nxt // NGY, nxt % NGY)
    up, down = (dev + NY) % total, (dev + total - NY) % total
    up_id = (up // NGY, up % NGY)
    down_id = (down // NGY, down % NGY)

    def reach(axis, steps):
        if axis == "y":
            return gx, z * NY + (y + steps) % NY
        return gx, ((z + steps) % NZ) * NY + y


    loads = [
        pltpu.make_async_copy(s, d, in_sem.at[i])
        for i, (s, d) in enumerate(
            [
                (ch_hbm, ch), (cnt_hbm, cnt), (basis_hbm, basis), (transfer_hbm, transfer),
                (nb_hbm, nb), (lp_hbm, lp), (pp_hbm, pp), (pc_hbm, pc), (lc_hbm, lc),
            ]
        )
    ]
    for load in loads:
        load.start()

    barrier = pltpu.get_barrier_semaphore()
    greeted = [reach(axis, steps) for axis, steps in REACH] + [prv_id, nxt_id, up_id, down_id]
    for d in greeted:
        pl.semaphore_signal(barrier, inc=1, device_id=d, device_id_type=MESH)

    mine, before, after = ((d % WIN) * QD for d in (dev, prv, nxt))

    lane = lax.broadcasted_iota(jnp.int32, (R, 128), 1)
    low = lane < 64

    def masks(q):
        return lane < cnt[2 * q], (lane >= 64) & (lane < cnt[2 * q + 1] + 64)

    def swap(tile):
        return jnp.concatenate([tile[:, 64:], tile[:, :64]], axis=1)

    for load in loads[:4]:
        load.wait()

    zero = jnp.zeros((R, 128), BF)
    parents = []
    for q in range(QD):
        m0, m1 = masks(q)
        tile = ch[:, 128 * q : 128 * q + 128]
        l0 = jnp.where(m0, tile, zero)
        l1 = jnp.where(m1, tile, zero)
        live[q + 1] = l0 + l1
        coef = dot_nn(jnp.concatenate([l0, l1], axis=0), basis[2 * q : 2 * q + 2].reshape(128, 64))
        coef = coef.astype(BF)
        pair = jnp.concatenate([coef[:R], coef[R:]], axis=1)
        win[0, mine + q] = pair
        win[1, mine + q] = jnp.concatenate([coef[R:], coef[:R]], axis=1)
        parents.append(dot_nn(pair, transfer[2 * q : 2 * q + 2].reshape(128, 64)).astype(BF))
        if q % 2:
            a, b = parents[q - 1], parents[q]
            at = pl.ds(gy * UD + q - 1, 2)
            row[0, at] = jnp.concatenate([a, b], axis=1).reshape(2, 16, 128)
            row[1, at] = jnp.concatenate([b, a], axis=1).reshape(2, 16, 128)

    pl.semaphore_wait(barrier, len(greeted))

    def rows_of(dy, dz, part):
        start, size = SPAN[part]
        origin = ((z + (NZ - dz)) % NZ) * NY + (y + (NY - dy)) % NY
        return pl.ds(origin * UD + start, size)

    def copy_of(rows, m, to):
        ref = row.at[0, rows]
        return pltpu.make_async_remote_copy(
            src_ref=ref, dst_ref=ref, send_sem=send_sem, recv_sem=recv_sem.at[NUMBER[m]],
            device_id=to, device_id_type=MESH,
        )

    def send_on(dy, dz, part):
        for d, steps, m in ROUTES.get((dy, dz, part), ()):
            steps = steps if d[1] == "+" else (NY if d[0] == "y" else NZ) - steps
            copy_of(rows_of(dy, dz, m[2]), m, reach(d[0], steps)).start()

    def receive(m):
        copy_of(rows_of(*m), m, greeted[0]).wait_recv()

    for d, steps, m in FIRST:
        steps = steps if d[1] == "+" else (NY if d[0] == "y" else NZ) - steps
        copy_of(rows_of(0, 0, m[2]), m, reach(d[0], steps)).start()

    def rim_part(i):
        return win.at[0, pl.ds(mine + i * RIM, RIM)]

    rims = [
        pltpu.make_async_remote_copy(
            src_ref=s, dst_ref=d, send_sem=rim_send.at[i], recv_sem=rim_recv.at[i],
            device_id=to, device_id_type=MESH,
        )
        for i, (s, d, to) in enumerate(
            [
                (live.at[pl.ds(QD, 1)], live.at[pl.ds(0, 1)], nxt_id),
                (live.at[pl.ds(1, 1)], live.at[pl.ds(QD + 1, 1)], prv_id),
            ]
            + [
                (rim_part(j), rim_part(j), to)
                for j in range(QD // RIM)
                for to in (nxt_id, prv_id)
            ]
        )
    ]
    def detour(j, forward):
        k = 2 + 2 * j + (0 if forward else 1)
        some = dev != (total - 1 if forward else 0)
        far = y == (NY - 1 if forward else 0)
        held_there = (y == (0 if forward else NY - 1)) & (dev != (total - NY if forward else NY - 1))
        slot = ((NY - 1) if forward else 0) * QD + j * RIM
        part = relay.at[pl.ds(j * RIM, RIM)]
        there = pltpu.make_async_remote_copy(
            src_ref=rim_part(j), dst_ref=part, send_sem=rim_send.at[k],
            recv_sem=relay_recv.at[j], device_id=reach("y", 1 if forward else NY - 1),
            device_id_type=MESH,
        )
        onward = pltpu.make_async_remote_copy(
            src_ref=part, dst_ref=win.at[0, pl.ds(slot, RIM)], send_sem=relay_send.at[j],
            recv_sem=rim_recv.at[k], device_id=up_id if forward else down_id,
            device_id_type=MESH,
        )
        return rims[k], some & jnp.logical_not(far), some & far, there, held_there, onward

    detours = [detour(j, forward) for j in range(2) for forward in (True, False)]

    def start_rims(step):
        for j, at in enumerate(RIM_AT):
            if at == step and j >= 2:
                for k in (2 + 2 * j, 3 + 2 * j):
                    pl.when(dev != (total - 1 if k % 2 == 0 else 0))(rims[k].start)
            elif at == step:
                for straight, near_by, far, there, _, _ in detours[2 * j : 2 * j + 2]:
                    pl.when(far)(there.start)
                    pl.when(near_by)(straight.start)
        if step == -1:
            for k in range(2):
                pl.when(dev != (total - 1 if k % 2 == 0 else 0))(rims[k].start)
        if step == RELAY_AT:
            for _, _, _, there, held_there, onward in detours:

                @pl.when(held_there)
                def _(there=there, onward=onward):
                    there.wait_recv()
                    onward.start()

    start_rims(-1)

    def do_diag(q):
        b0, b1 = basis[2 * q], basis[2 * q + 1]
        o = jnp.zeros((64, 64), BF)
        both = [jnp.concatenate([b0, o], axis=1), jnp.concatenate([o, b1], axis=1)]
        bdiag[q] = jnp.concatenate(both, axis=0).T

    def do_near(q):
        o = jnp.zeros((64, 64), BF)
        o2 = jnp.zeros((64, 128), BF)
        top = jnp.concatenate([o, nb[2 * q, 0], nb[2 * q, 1], nb[2 * q, 2], o2], axis=1)
        low_rows = jnp.concatenate(
            [o2, nb[2 * q + 1, 0], nb[2 * q + 1, 1], nb[2 * q + 1, 2], o], axis=1
        )
        lhs = jnp.concatenate([live[q], live[q + 1], live[q + 2]], axis=1)
        near[q] = dot_nt(lhs, jnp.concatenate([top, low_rows], axis=0))

    def do_couple(q):
        for i in range(8):
            cpl[q, :, 128 * i : 128 * i + 128] = jnp.concatenate(
                [pc[q, 2 * i], pc[q, 2 * i + 1]], axis=1
            )

    def pick_leaves(p, q):
        a = win[p & 1, (p >> 1) & (WIN * QD - 1)]
        b = win[1 - (q & 1), (q >> 1) & (WIN * QD - 1)]
        return jnp.where(low, a, b)

    def pick_parents(p, q):
        a = (p >> 1) & (ROW_UNITS // 2 - 1)
        b = (q >> 1) & (ROW_UNITS // 2 - 1)
        return jnp.concatenate(
            [
                jnp.where(low[:16], row[p & 1, 2 * a + i], row[1 - (q & 1), 2 * b + i])
                for i in range(2)
            ],
            axis=0,
        )

    def leaf_sum(g):
        lhs = jnp.concatenate(
            [pick_leaves(lp[2 * i, g], lp[2 * i + 1, g]) for i in range(8)], axis=1
        )
        rhs = jnp.concatenate([lc[g, j] for j in range(16)], axis=1)
        return dot_nt(lhs, rhs)

    def do_far(q):
        far[q] = jnp.concatenate([leaf_sum(2 * q), leaf_sum(2 * q + 1)], axis=1)

    def take_rims():
        for k, rim in enumerate(rims):
            pl.when(dev != (0 if k % 2 == 0 else total - 1))(rim.wait_recv)
        live[0] = jnp.where(dev > 0, live[0], zero)
        live[QD + 1] = jnp.where(dev < total - 1, live[QD + 1], zero)

        @pl.loop(0, QD)
        def _(t):
            win[1, before + t] = swap(win[0, before + t])
            win[1, after + t] = swap(win[0, after + t])

    def wait_load(i):
        return loads[i].wait

    work = [lambda q=q: do_diag(q) for q in range(QD)]
    work += [wait_load(4)] + [lambda q=q: do_near(q) for q in range(1, QD - 1)]
    work += [wait_load(7)] + [lambda q=q: do_couple(q) for q in range(QD)]
    work += [wait_load(5), wait_load(8), take_rims]
    work += [lambda: do_near(0), lambda: do_near(QD - 1)]
    work += [lambda q=q: do_far(q) for q in range(QD)]
    todo = iter(work)

    def do_work(n):
        for _ in range(n):
            next(todo, lambda: None)()

    do_work(FIRST_WORK)
    for number, (step, pieces) in enumerate(STEPS):
        for m in step:
            receive(m)
        dy, dz, part = step[0]
        send_on(dy, dz, part[0] if len(step) == 2 else part)
        start_rims(number)
        for m in step:
            rows = rows_of(*m)
            n = SPAN[m[2]][1]
            row[1, rows] = swap(row[0, rows].reshape(n * 16, 128)).reshape(n, 16, 128)
        do_work(pieces)
    for unit in todo:
        unit()

    loads[6].wait()
    for q in range(QD):
        lhs = jnp.concatenate(
            [pick_parents(pp[q, 2 * i], pp[q, 2 * i + 1]) for i in range(8)], axis=1
        )
        held[q] = dot_nt(lhs, cpl[q]).astype(BF)
    for q in range(QD):
        local = dot_nt(held[q], transfer[2 * q : 2 * q + 2].reshape(128, 64)) + far[q]
        coefs[q] = local.astype(BF)
    for q in range(QD):
        total_q = dot_nn(coefs[q], bdiag[q]) + near[q]
        m0, m1 = masks(q)
        out_ref[:, 128 * q : 128 * q + 128] = jnp.where(m0 | m1, total_q, 0.0).astype(BF)

    for k, rim in enumerate(rims):
        pl.when(dev != (total - 1 if k % 2 == 0 else 0))(rim.wait_send)
    for _, _, _, _, held_there, onward in detours:
        pl.when(held_there)(onward.wait_send)
    copy_of(pl.ds(0, ROW_UNITS - UD), MESSAGES[0], greeted[0]).wait_send()


def per_device(
    charges, panel_counts, basis, transfer, leaf_coupling, leaf_partners, near_blocks,
    parent_coupling, parent_partners,
):
    n = charges.shape[0]
    result = pl.pallas_call(
        kernel,
        out_shape=pltpu.VMEM((R, n), BF),
        in_specs=[pl.BlockSpec(memory_space=pltpu.HBM)] * 9,
        out_specs=pl.BlockSpec(memory_space=pltpu.VMEM),
        scratch_shapes=[
            pltpu.VMEM((R, n), BF),
            pltpu.VMEM(basis.shape, BF),
            pltpu.VMEM(transfer.shape, BF),
            pltpu.VMEM(leaf_coupling.shape, BF),
            pltpu.VMEM(near_blocks.shape, BF),
            pltpu.VMEM(parent_coupling.shape, BF),
            pltpu.SMEM((LD,), jnp.int32),
            pltpu.SMEM((16, LD), jnp.int32),
            pltpu.SMEM((QD, 16), jnp.int32),
            pltpu.VMEM((QD + 2, R, 128), BF),
            pltpu.VMEM((2, WIN * QD, R, 128), BF),
            pltpu.VMEM((2, ROW_UNITS, 16, 128), BF),
            pltpu.VMEM((QD, 64, 1024), BF),
            pltpu.VMEM((QD, 128, 128), BF),
            pltpu.VMEM((QD, R, 128), F32),
            pltpu.VMEM((QD, R, 128), F32),
            pltpu.VMEM((QD, R, 64), BF),
            pltpu.VMEM((QD, R, 128), BF),
            pltpu.VMEM((2 * RIM, R, 128), BF),
            pltpu.SemaphoreType.DMA((9,)),
            pltpu.SemaphoreType.DMA((len(MESSAGES),)),
            pltpu.SemaphoreType.DMA,
            pltpu.SemaphoreType.DMA((2 + 2 * QD // RIM,)),
            pltpu.SemaphoreType.DMA((2 + 2 * QD // RIM,)),
            pltpu.SemaphoreType.DMA((2,)),
            pltpu.SemaphoreType.DMA((2,)),
        ],
        compiler_params=pltpu.CompilerParams(
            collective_id=0, has_side_effects=True, vmem_limit_bytes=56 * 1024 * 1024
        ),
    )(
        charges.T, panel_counts, basis, transfer, leaf_coupling, leaf_partners.T, near_blocks,
        parent_coupling, parent_partners,
    )
    return result.T


def solution(mesh):
    in_specs = (
        P(("gx", "gy"), None),
        P(("gx", "gy")),
        P(("gx", "gy"), None, None),
        P(("gx", "gy"), None, None),
        P(("gx", "gy"), None, None, None),
        P(("gx", "gy"), None),
        P(("gx", "gy"), None, None, None),
        P(("gx", "gy"), None, None, None),
        P(("gx", "gy"), None),
    )
    out_specs = P(("gx", "gy"), None)
    return jax.shard_map(
        per_device, mesh=mesh, in_specs=in_specs, out_specs=out_specs, check_vma=False
    )
```

```python
import jax
import jax.numpy as jnp
from jax import lax
from jax.experimental import pallas as pl
from jax.experimental.pallas import tpu as pltpu
from jax.sharding import PartitionSpec as P

BF = jnp.bfloat16
F32 = jnp.float32
MESH = pl.DeviceIdType.MESH

NY = 4
NZ = 8
NGX = 8
NGY = NY * NZ
LD = 32
QD = 16
UD = QD
ROW_UNITS = NGY * UD
R = 32
WIN = 4
RIM = 4

SPAN = {"A": (0, 7), "A0": (0, 4), "A1": (4, 3), "B": (7, 9), "B0": (7, 5), "B1": (12, 4)}

FIRST = (
    ("z+", 2, (0, 2, "B")),
    ("y+", 1, (1, 0, "B")),
    ("y+", 2, (2, 0, "A0")),
    ("z-", 2, (0, -2, "B")),
    ("y-", 2, (2, 0, "A1")),
    ("z-", 1, (0, -1, "B")),
    ("z+", 1, (0, 1, "B")),
    ("y-", 1, (-1, 0, "A")),
    ("y-", 1, (-1, 0, "B")),
    ("z+", 1, (0, 1, "A")),
    ("z-", 1, (0, -1, "A")),
    ("y+", 1, (1, 0, "A")),
)

ROUTES = {
    (1, 0, "B"): (("y+", 1, (2, 0, "B0")),),
    (-1, 0, "A"): (("z+", 1, (-1, 1, "A")), ("z-", 1, (-1, -1, "A"))),
    (0, 1, "B"): (("y+", 1, (1, 1, "B")), ("y-", 1, (-1, 1, "B"))),
    (0, -1, "B"): (("y+", 1, (1, -1, "B")), ("y-", 1, (-1, -1, "B"))),
    (1, 0, "A"): (("z+", 1, (1, 1, "A")), ("z-", 1, (1, -1, "A"))),
    (-1, 0, "B"): (("y-", 1, (2, 0, "B1")),),
    (0, 1, "A"): (("z+", 1, (0, 2, "A")),),
    (0, -1, "A"): (("z-", 1, (0, -2, "A")),),
    (0, 2, "B"): (("z+", 1, (0, 3, "B")), ("y+", 1, (1, 2, "B")), ("y-", 1, (-1, 2, "B"))),
    (0, -2, "B"): (("z-", 1, (0, -3, "B")), ("y+", 1, (1, -2, "B")), ("y-", 1, (-1, -2, "B"))),
    (2, 0, "A"): (("z+", 1, (2, 1, "A")), ("z-", 1, (2, -1, "A"))),
    (-1, 1, "A"): (("z+", 1, (-1, 2, "A")),),
    (-1, -1, "A"): (("z-", 1, (-1, -2, "A")),),
    (-1, 1, "B"): (("y-", 1, (2, 1, "B1")),),
    (1, 1, "B"): (("y+", 1, (2, 1, "B0")),),
    (1, 1, "A"): (("z+", 1, (1, 2, "A")),),
    (1, -1, "A"): (("z-", 1, (1, -2, "A")),),
    (0, 2, "A"): (("z+", 1, (0, 3, "A")),),
    (-1, -1, "B"): (("y-", 1, (2, -1, "B1")),),
    (1, -1, "B"): (("y+", 1, (2, -1, "B0")),),
    (0, -2, "A"): (("z-", 1, (0, -3, "A")),),
    (0, 3, "B"): (("z+", 1, (0, 4, "B0")), ("y+", 1, (1, 3, "B")), ("y-", 1, (-1, 3, "B"))),
    (1, 2, "B"): (("y+", 1, (2, 2, "B0")),),
    (0, -3, "B"): (("z-", 1, (0, 4, "B1")), ("y+", 1, (1, -3, "B")), ("y-", 1, (-1, -3, "B"))),
    (-1, 2, "B"): (("y-", 1, (2, 2, "B1")),),
    (2, 1, "A"): (("z+", 1, (2, 2, "A")),),
    (2, -1, "A"): (("z-", 1, (2, -2, "A")),),
    (1, -2, "B"): (("y+", 1, (2, -2, "B0")),),
    (-1, 2, "A"): (("z+", 1, (-1, 3, "A")),),
    (-1, -2, "A"): (("z-", 1, (-1, -3, "A")),),
    (-1, -2, "B"): (("y-", 1, (2, -2, "B1")),),
    (1, 2, "A"): (("z+", 1, (1, 3, "A")),),
    (1, -2, "A"): (("z-", 1, (1, -3, "A")),),
    (0, 3, "A"): (("z+", 1, (0, 4, "A0")),),
    (0, -3, "A"): (("z-", 1, (0, 4, "A1")),),
    (0, 4, "B"): (("y+", 2, (2, 4, "B0")), ("y-", 2, (2, 4, "B1")), ("y+", 1, (1, 4, "B")), ("y-", 1, (-1, 4, "B"))),
    (1, 3, "B"): (("y+", 1, (2, 3, "B0")),),
    (-1, 3, "B"): (("y-", 1, (2, 3, "B1")),),
    (2, 2, "A"): (("z+", 2, (2, 4, "A0")), ("z+", 1, (2, 3, "A"))),
    (2, -2, "A"): (("z-", 2, (2, 4, "A1")), ("z-", 1, (2, -3, "A"))),
    (-1, 3, "A"): (("z+", 1, (-1, 4, "A0")),),
    (-1, -3, "A"): (("z-", 1, (-1, 4, "A1")),),
    (-1, -3, "B"): (("y-", 1, (2, -3, "B1")),),
    (1, -3, "B"): (("y+", 1, (2, -3, "B0")),),
    (1, 3, "A"): (("z+", 1, (1, 4, "A0")),),
    (1, -3, "A"): (("z-", 1, (1, 4, "A1")),),
}

RIM_AT = (-1, -1, 8, 16)
FIRST_WORK = 50
STEPS = (
    (((1, 0, "B"),), 0),
    (((-1, 0, "A"),), 0),
    (((0, 1, "B"),), 0),
    (((0, -1, "B"),), 0),
    (((1, 0, "A"),), 0),
    (((-1, 0, "B"),), 0),
    (((0, 1, "A"),), 0),
    (((0, -1, "A"),), 0),
    (((0, 2, "B"),), 0),
    (((0, -2, "B"),), 0),
    (((2, 0, "A0"), (2, 0, "A1")), 0),
    (((-1, 1, "A"),), 0),
    (((-1, -1, "A"),), 0),
    (((-1, 1, "B"),), 0),
    (((1, 1, "B"),), 0),
    (((1, 1, "A"),), 0),
    (((1, -1, "A"),), 0),
    (((0, 2, "A"),), 0),
    (((-1, -1, "B"),), 0),
    (((1, -1, "B"),), 0),
    (((0, -2, "A"),), 0),
    (((2, 0, "B0"), (2, 0, "B1")), 0),
    (((0, 3, "B"),), 0),
    (((1, 2, "B"),), 0),
    (((0, -3, "B"),), 0),
    (((-1, 2, "B"),), 0),
    (((2, 1, "A"),), 0),
    (((2, -1, "A"),), 0),
    (((1, -2, "B"),), 0),
    (((-1, 2, "A"),), 0),
    (((-1, -2, "A"),), 0),
    (((-1, -2, "B"),), 0),
    (((1, 2, "A"),), 0),
    (((2, 1, "B0"), (2, 1, "B1")), 0),
    (((1, -2, "A"),), 0),
    (((0, 3, "A"),), 0),
    (((0, -3, "A"),), 0),
    (((2, -1, "B0"), (2, -1, "B1")), 0),
    (((0, 4, "B0"), (0, 4, "B1")), 0),
    (((1, 3, "B"),), 0),
    (((-1, 3, "B"),), 8),
    (((2, 2, "A"),), 0),
    (((2, -2, "A"),), 0),
    (((-1, 3, "A"),), 0),
    (((-1, -3, "A"),), 0),
    (((-1, -3, "B"),), 0),
    (((1, -3, "B"),), 0),
    (((2, 2, "B0"), (2, 2, "B1")), 2),
    (((1, 3, "A"),), 0),
    (((1, -3, "A"),), 0),
    (((2, -2, "B0"), (2, -2, "B1")), 0),
    (((0, 4, "A0"), (0, 4, "A1")), 9),
    (((-1, 4, "B"),), 0),
    (((1, 4, "B"),), 0),
    (((2, 3, "A"),), 0),
    (((2, -3, "A"),), 0),
    (((2, 3, "B0"), (2, 3, "B1")), 0),
    (((-1, 4, "A0"), (-1, 4, "A1")), 0),
    (((2, 4, "B0"), (2, 4, "B1")), 0),
    (((2, 4, "A0"), (2, 4, "A1")), 0),
    (((2, -3, "B0"), (2, -3, "B1")), 0),
    (((1, 4, "A0"), (1, 4, "A1")), 0),
)

RELAY_AT = 12
MESSAGES = tuple(m for step, _ in STEPS for m in step)
REACH = tuple(sorted({(d[0], h * (1 if d[1] == "+" else -1) % (NY if d[0] == "y" else NZ)) for out in (FIRST, *ROUTES.values()) for d, h, _ in out}))
NUMBER = {m: i for i, m in enumerate(MESSAGES)}


def dot_nn(a, b):
    return lax.dot_general(a, b, (((1,), (0,)), ((), ())), preferred_element_type=F32)


def dot_nt(a, b):
    return lax.dot_general(a, b, (((1,), (1,)), ((), ())), preferred_element_type=F32)


def kernel(
    ch_hbm, cnt_hbm, basis_hbm, transfer_hbm, lc_hbm, lp_hbm, nb_hbm, pc_hbm, pp_hbm,
    out_ref,
    ch, basis, transfer, lc, nb, pc, cnt, lp, pp,
    live, win, row, cpl, bdiag, near, far, held, coefs, down_t,
    relay, in_sem, recv_sem, send_sem, rim_recv, rim_send, relay_recv, relay_send,
):
    gx = lax.axis_index("gx")
    gy = lax.axis_index("gy")
    z = gy // NY
    y = gy % NY
    dev = gx * NGY + gy
    total = NGX * NGY
    prv = (dev + total - 1) % total
    nxt = (dev + 1) % total
    prv_id = (prv // NGY, prv % NGY)
    nxt_id = (nxt // NGY, nxt % NGY)
    up, down = (dev + NY) % total, (dev + total - NY) % total
    up_id = (up // NGY, up % NGY)
    down_id = (down // NGY, down % NGY)

    def reach(axis, steps):
        if axis == "y":
            return gx, z * NY + (y + steps) % NY
        return gx, ((z + steps) % NZ) * NY + y


    loads = [
        pltpu.make_async_copy(s, d, in_sem.at[i])
        for i, (s, d) in enumerate(
            [
                (ch_hbm, ch), (cnt_hbm, cnt), (basis_hbm, basis), (transfer_hbm, transfer),
                (nb_hbm, nb), (lp_hbm, lp), (pp_hbm, pp), (pc_hbm, pc), (lc_hbm, lc),
            ]
        )
    ]
    for load in loads:
        load.start()

    barrier = pltpu.get_barrier_semaphore()
    greeted = [reach(axis, steps) for axis, steps in REACH] + [prv_id, nxt_id, up_id, down_id]
    for d in greeted:
        pl.semaphore_signal(barrier, inc=1, device_id=d, device_id_type=MESH)

    mine, before, after = ((d % WIN) * QD for d in (dev, prv, nxt))

    lane = lax.broadcasted_iota(jnp.int32, (R, 128), 1)
    low = lane < 64

    def masks(q):
        return lane < cnt[2 * q], (lane >= 64) & (lane < cnt[2 * q + 1] + 64)

    def swap(tile):
        return jnp.concatenate([tile[:, 64:], tile[:, :64]], axis=1)

    for load in loads[:4]:
        load.wait()

    zero = jnp.zeros((R, 128), BF)
    parents = []
    for q in range(QD):
        m0, m1 = masks(q)
        tile = ch[:, 128 * q : 128 * q + 128]
        l0 = jnp.where(m0, tile, zero)
        l1 = jnp.where(m1, tile, zero)
        live[q + 1] = l0 + l1
        coef = dot_nn(jnp.concatenate([l0, l1], axis=0), basis[2 * q : 2 * q + 2].reshape(128, 64))
        coef = coef.astype(BF)
        pair = jnp.concatenate([coef[:R], coef[R:]], axis=1)
        win[0, mine + q] = pair
        win[1, mine + q] = jnp.concatenate([coef[R:], coef[:R]], axis=1)
        parents.append(dot_nn(pair, transfer[2 * q : 2 * q + 2].reshape(128, 64)).astype(BF))
        if q % 2:
            a, b = parents[q - 1], parents[q]
            at = pl.ds(gy * UD + q - 1, 2)
            row[0, at] = jnp.concatenate([a, b], axis=1).reshape(2, 16, 128)
            row[1, at] = jnp.concatenate([b, a], axis=1).reshape(2, 16, 128)

    pl.semaphore_wait(barrier, len(greeted))

    def rows_of(dy, dz, part):
        start, size = SPAN[part]
        origin = ((z + (NZ - dz)) % NZ) * NY + (y + (NY - dy)) % NY
        return pl.ds(origin * UD + start, size)

    def copy_of(rows, m, to):
        ref = row.at[0, rows]
        return pltpu.make_async_remote_copy(
            src_ref=ref, dst_ref=ref, send_sem=send_sem, recv_sem=recv_sem.at[NUMBER[m]],
            device_id=to, device_id_type=MESH,
        )

    def send_on(dy, dz, part):
        for d, steps, m in ROUTES.get((dy, dz, part), ()):
            steps = steps if d[1] == "+" else (NY if d[0] == "y" else NZ) - steps
            copy_of(rows_of(dy, dz, m[2]), m, reach(d[0], steps)).start()

    def receive(m):
        copy_of(rows_of(*m), m, greeted[0]).wait_recv()

    for d, steps, m in FIRST:
        steps = steps if d[1] == "+" else (NY if d[0] == "y" else NZ) - steps
        copy_of(rows_of(0, 0, m[2]), m, reach(d[0], steps)).start()

    def rim_part(i):
        return win.at[0, pl.ds(mine + i * RIM, RIM)]

    rims = [
        pltpu.make_async_remote_copy(
            src_ref=s, dst_ref=d, send_sem=rim_send.at[i], recv_sem=rim_recv.at[i],
            device_id=to, device_id_type=MESH,
        )
        for i, (s, d, to) in enumerate(
            [
                (live.at[pl.ds(QD, 1)], live.at[pl.ds(0, 1)], nxt_id),
                (live.at[pl.ds(1, 1)], live.at[pl.ds(QD + 1, 1)], prv_id),
            ]
            + [
                (rim_part(j), rim_part(j), to)
                for j in range(QD // RIM)
                for to in (nxt_id, prv_id)
            ]
        )
    ]
    def detour(j, forward):
        k = 2 + 2 * j + (0 if forward else 1)
        some = dev != (total - 1 if forward else 0)
        far = y == (NY - 1 if forward else 0)
        held_there = (y == (0 if forward else NY - 1)) & (dev != (total - NY if forward else NY - 1))
        slot = ((NY - 1) if forward else 0) * QD + j * RIM
        part = relay.at[pl.ds(j * RIM, RIM)]
        there = pltpu.make_async_remote_copy(
            src_ref=rim_part(j), dst_ref=part, send_sem=rim_send.at[k],
            recv_sem=relay_recv.at[j], device_id=reach("y", 1 if forward else NY - 1),
            device_id_type=MESH,
        )
        onward = pltpu.make_async_remote_copy(
            src_ref=part, dst_ref=win.at[0, pl.ds(slot, RIM)], send_sem=relay_send.at[j],
            recv_sem=rim_recv.at[k], device_id=up_id if forward else down_id,
            device_id_type=MESH,
        )
        return rims[k], some & jnp.logical_not(far), some & far, there, held_there, onward

    detours = [detour(j, forward) for j in range(2) for forward in (True, False)]

    def start_rims(step):
        for j, at in enumerate(RIM_AT):
            if at == step and j >= 2:
                for k in (2 + 2 * j, 3 + 2 * j):
                    pl.when(dev != (total - 1 if k % 2 == 0 else 0))(rims[k].start)
            elif at == step:
                for straight, near_by, far, there, _, _ in detours[2 * j : 2 * j + 2]:
                    pl.when(far)(there.start)
                    pl.when(near_by)(straight.start)
        if step == -1:
            for k in range(2):
                pl.when(dev != (total - 1 if k % 2 == 0 else 0))(rims[k].start)
        if step == RELAY_AT:
            for _, _, _, there, held_there, onward in detours:

                @pl.when(held_there)
                def _(there=there, onward=onward):
                    there.wait_recv()
                    onward.start()

    start_rims(-1)

    def do_diag(q):
        b0, b1 = basis[2 * q], basis[2 * q + 1]
        o = jnp.zeros((64, 64), BF)
        both = [jnp.concatenate([b0, o], axis=1), jnp.concatenate([o, b1], axis=1)]
        bdiag[q] = jnp.concatenate(both, axis=0).T
        down_t[q] = transfer[2 * q : 2 * q + 2].reshape(128, 64).T

    def do_near(q):
        o = jnp.zeros((64, 64), BF)
        o2 = jnp.zeros((64, 128), BF)
        top = jnp.concatenate([o, nb[2 * q, 0], nb[2 * q, 1], nb[2 * q, 2], o2], axis=1)
        low_rows = jnp.concatenate(
            [o2, nb[2 * q + 1, 0], nb[2 * q + 1, 1], nb[2 * q + 1, 2], o], axis=1
        )
        lhs = jnp.concatenate([live[q], live[q + 1], live[q + 2]], axis=1)
        near[q] = dot_nt(lhs, jnp.concatenate([top, low_rows], axis=0))

    def do_couple(q):
        for i in range(8):
            cpl[q, :, 128 * i : 128 * i + 128] = jnp.concatenate(
                [pc[q, 2 * i], pc[q, 2 * i + 1]], axis=1
            )

    def pick_leaves(p, q):
        a = win[p & 1, (p >> 1) & (WIN * QD - 1)]
        b = win[1 - (q & 1), (q >> 1) & (WIN * QD - 1)]
        return jnp.where(low, a, b)

    def pick_parents(p, q):
        a = (p >> 1) & (ROW_UNITS // 2 - 1)
        b = (q >> 1) & (ROW_UNITS // 2 - 1)
        return jnp.concatenate(
            [
                jnp.where(low[:16], row[p & 1, 2 * a + i], row[1 - (q & 1), 2 * b + i])
                for i in range(2)
            ],
            axis=0,
        )

    def leaf_sum(g):
        lhs = jnp.concatenate(
            [pick_leaves(lp[2 * i, g], lp[2 * i + 1, g]) for i in range(8)], axis=1
        )
        rhs = jnp.concatenate([lc[g, j] for j in range(16)], axis=1)
        return dot_nt(lhs, rhs)

    def do_far(q):
        far[q] = jnp.concatenate([leaf_sum(2 * q), leaf_sum(2 * q + 1)], axis=1)

    def take_rims():
        for k, rim in enumerate(rims):
            pl.when(dev != (0 if k % 2 == 0 else total - 1))(rim.wait_recv)
        live[0] = jnp.where(dev > 0, live[0], zero)
        live[QD + 1] = jnp.where(dev < total - 1, live[QD + 1], zero)

        @pl.loop(0, QD)
        def _(t):
            win[1, before + t] = swap(win[0, before + t])
            win[1, after + t] = swap(win[0, after + t])

    def wait_load(i):
        return loads[i].wait

    work = [lambda q=q: do_diag(q) for q in range(QD)]
    work += [wait_load(4)] + [lambda q=q: do_near(q) for q in range(1, QD - 1)]
    work += [wait_load(7)] + [lambda q=q: do_couple(q) for q in range(QD)]
    work += [wait_load(5), wait_load(8), take_rims]
    work += [lambda: do_near(0), lambda: do_near(QD - 1)]
    work += [lambda q=q: do_far(q) for q in range(QD)]
    todo = iter(work)

    def do_work(n):
        for _ in range(n):
            next(todo, lambda: None)()

    do_work(FIRST_WORK)
    for number, (step, pieces) in enumerate(STEPS):
        for m in step:
            receive(m)
        dy, dz, part = step[0]
        send_on(dy, dz, part[0] if len(step) == 2 else part)
        start_rims(number)
        for m in step:
            rows = rows_of(*m)
            n = SPAN[m[2]][1]
            row[1, rows] = swap(row[0, rows].reshape(n * 16, 128)).reshape(n, 16, 128)
        do_work(pieces)
        if number == len(STEPS) - 5:
            loads[6].wait()
            for k, rim in enumerate(rims):
                pl.when(dev != (total - 1 if k % 2 == 0 else 0))(rim.wait_send)
            for _, _, _, _, held_there, onward in detours:
                pl.when(held_there)(onward.wait_send)
    for unit in todo:
        unit()

    for q in range(QD):
        lhs = jnp.concatenate(
            [pick_parents(pp[q, 2 * i], pp[q, 2 * i + 1]) for i in range(8)], axis=1
        )
        held[q] = dot_nt(lhs, cpl[q]).astype(BF)
    for q in range(QD):
        local = dot_nn(held[q], down_t[q]) + far[q]
        coefs[q] = local.astype(BF)
    for q in range(QD):
        total_q = dot_nn(coefs[q], bdiag[q]) + near[q]
        m0, m1 = masks(q)
        out_ref[:, 128 * q : 128 * q + 128] = jnp.where(m0 | m1, total_q, 0.0).astype(BF)

    copy_of(pl.ds(0, ROW_UNITS - UD), MESSAGES[0], greeted[0]).wait_send()


def per_device(
    charges, panel_counts, basis, transfer, leaf_coupling, leaf_partners, near_blocks,
    parent_coupling, parent_partners,
):
    n = charges.shape[0]
    result = pl.pallas_call(
        kernel,
        out_shape=pltpu.VMEM((R, n), BF),
        in_specs=[pl.BlockSpec(memory_space=pltpu.HBM)] * 9,
        out_specs=pl.BlockSpec(memory_space=pltpu.VMEM),
        scratch_shapes=[
            pltpu.VMEM((R, n), BF),
            pltpu.VMEM(basis.shape, BF),
            pltpu.VMEM(transfer.shape, BF),
            pltpu.VMEM(leaf_coupling.shape, BF),
            pltpu.VMEM(near_blocks.shape, BF),
            pltpu.VMEM(parent_coupling.shape, BF),
            pltpu.SMEM((LD,), jnp.int32),
            pltpu.SMEM((16, LD), jnp.int32),
            pltpu.SMEM((QD, 16), jnp.int32),
            pltpu.VMEM((QD + 2, R, 128), BF),
            pltpu.VMEM((2, WIN * QD, R, 128), BF),
            pltpu.VMEM((2, ROW_UNITS, 16, 128), BF),
            pltpu.VMEM((QD, 64, 1024), BF),
            pltpu.VMEM((QD, 128, 128), BF),
            pltpu.VMEM((QD, R, 128), F32),
            pltpu.VMEM((QD, R, 128), F32),
            pltpu.VMEM((QD, R, 64), BF),
            pltpu.VMEM((QD, R, 128), BF),
            pltpu.VMEM((QD, 64, 128), BF),
            pltpu.VMEM((2 * RIM, R, 128), BF),
            pltpu.SemaphoreType.DMA((9,)),
            pltpu.SemaphoreType.DMA((len(MESSAGES),)),
            pltpu.SemaphoreType.DMA,
            pltpu.SemaphoreType.DMA((2 + 2 * QD // RIM,)),
            pltpu.SemaphoreType.DMA((2 + 2 * QD // RIM,)),
            pltpu.SemaphoreType.DMA((2,)),
            pltpu.SemaphoreType.DMA((2,)),
        ],
        compiler_params=pltpu.CompilerParams(
            collective_id=0, has_side_effects=True, vmem_limit_bytes=56 * 1024 * 1024
        ),
    )(
        charges.T, panel_counts, basis, transfer, leaf_coupling, leaf_partners.T, near_blocks,
        parent_coupling, parent_partners,
    )
    return result.T


def solution(mesh):
    in_specs = (
        P(("gx", "gy"), None),
        P(("gx", "gy")),
        P(("gx", "gy"), None, None),
        P(("gx", "gy"), None, None),
        P(("gx", "gy"), None, None, None),
        P(("gx", "gy"), None),
        P(("gx", "gy"), None, None, None),
        P(("gx", "gy"), None, None, None),
        P(("gx", "gy"), None),
    )
    out_specs = P(("gx", "gy"), None)
    return jax.shard_map(
        per_device, mesh=mesh, in_specs=in_specs, out_specs=out_specs, check_vma=False
    )
```
